32 devices in a mesh: wide: 8 (over z, y), narrow: 4 (over x, core).
Axes of the slice: x: 2, y: 2, z: 4, core: 2. Of those that a mesh axis runs over, the one named last changes fastest.
Arguments:
- prefit_resid: float32 [1310720], P(('wide', 'narrow')), may hold values from -6 to 6
- source_partials: float32 [5, 1310720], P(None, ('wide', 'narrow')), may hold values from -6 to 6
- attitude_partials: float32 [4, 1310720], P(None, ('wide', 'narrow')), may hold values from -0.25 to 0.25
- spline_position: float32 [1310720], P(('wide', 'narrow')), may hold values from 0 to 1
- calib_partials: float32 [3, 1310720], P(None, ('wide', 'narrow')), may hold values from -2 to 2
- obs_source: int32 [1310720], P(('wide', 'narrow')), may hold values from 0 to 127
- block_count: int32 [2048], P(('wide', 'narrow')), may hold values from 320 to 640, as said below
- obs_range: int32 [1310720], P(('wide', 'narrow')), may hold values from 0 to 7, as said below
- obs_knot: int32 [1310720], P(('wide', 'narrow')), may hold values from 0 to 255
- obs_unit: int32 [1310720], P(('wide', 'narrow')), may hold values from 0 to 2015
- given_inverse: float32 [8, 1024, 1024], P('wide'), may hold values from -2.5 to 2.5, as said below
- knot_decay: float32 [4, 2048], P(None, 'wide'), may hold values from 0.15 to 1
Outputs:
- source_update: float32 [5, 262144], P(None, ('wide', 'narrow'))
- attitude_update: float32 [4, 2048], P(None, 'wide')
- cal_update: float32 [3, 2016], P(None, 'narrow')
The draws below stay inside these ranges and needn't reach their ends.
Inputs may be any that keep to these rules, and one draw needn't show every extreme that they name: `block_count`: each block's live observations are its first slots; every device has one block with all 640 slots live. `obs_range`: at most 10240 of one device's observation slots fall in one time range; for each index along narrow, some time range holds exactly 10240 slots of every device of that index. `given_inverse`: each time range's given inverse is symmetric.
All inputs are finite; a program needn't handle non-finite values.
Results may differ from the reference program's by a relative error of at most 0.0003.
Values sent between devices are 32-bit elements; how exact they have to be, the bound alone decides.
A program may use at most 64 MiB of HBM per device.

```python
import math
import jax
import jax.numpy as jnp
from jax import lax

SRC_BLK = 128
SLOT_BLK = 640
BLK_DEV = 64
KN_DEV = 256
RANGES = 8
GROUPS = 4
OBS_DEV = 40960
BLOCKS = 2048
SOURCES = 262144
OBS_TOTAL = 1310720
CAP = 10240
ATTITUDE_KNOTS = 2048
CAL = 2016
DEVICES = 32


def draw_block_count(key, part):
    counts = jax.random.randint(jax.random.fold_in(key, 1), (DEVICES, BLK_DEV), SLOT_BLK // 2, SLOT_BLK + 1)
    chosen = jax.random.randint(jax.random.fold_in(key, 2), (DEVICES, 1), 0, BLK_DEV)
    counts = jnp.where(jnp.arange(BLK_DEV, dtype=jnp.int32)[None, :] == chosen, SLOT_BLK, counts)
    return counts.reshape(BLOCKS).astype(jnp.int32)


def draw_obs_range(key, part):
    root_random_key = jax.random.fold_in(key, 7)
    favoured = jax.random.randint(jax.random.fold_in(root_random_key, 1), (GROUPS,), 0, RANGES)
    others_total = OBS_DEV - CAP
    base_load = others_total // (RANGES - 1)
    remainder = others_total - base_load * (RANGES - 1)
    paired = (RANGES - 1) // 2

    def one_device(device_at):
        device_key = jax.random.fold_in(root_random_key, device_at + 100)
        heavy = favoured[device_at % GROUPS]
        others = (heavy + 1 + jax.random.permutation(jax.random.fold_in(device_key, 1), RANGES - 1)) % RANGES
        order_list = jnp.concatenate([heavy[None], others]).astype(jnp.int32)
        moved = jax.random.randint(jax.random.fold_in(device_key, 2), (max(paired, 1),), 0, base_load // 2 + 1)[:paired]
        loads = jnp.full((RANGES - 1,), base_load, jnp.int32)
        loads = loads.at[0:2 * paired:2].add(moved).at[1:2 * paired:2].add(-moved)
        loads = loads.at[0].add(remainder)
        bounds = jnp.cumsum(jnp.concatenate([jnp.array([CAP], jnp.int32), loads]))
        places = jax.random.permutation(jax.random.fold_in(device_key, 3), OBS_DEV)
        picked = jnp.searchsorted(bounds, places, side='right')
        return order_list[picked]
    return jax.vmap(one_device)(jnp.arange(DEVICES, dtype=jnp.int32)).reshape(OBS_TOTAL).astype(jnp.int32)


def draw_given_inverse(key, part):
    order_size = 4 * KN_DEV
    key_noise = jax.random.fold_in(key, 1)
    key_diag = jax.random.fold_in(key, 2)
    noise = jax.random.normal(key_noise, (RANGES, order_size, order_size), jnp.float32)
    diagonal = jax.random.uniform(key_diag, (RANGES, order_size), jnp.float32, 0.8, 2.4)
    off_part = (noise + jnp.swapaxes(noise, 1, 2)) * (0.45 / math.sqrt(2.0 * order_size))
    identity = jnp.eye(order_size, dtype=jnp.float32)
    return (off_part * (1.0 - identity) + diagonal[:, :, None] * identity).astype(jnp.float32)


def draw_knot_decay(key, part):
    share_slow = 0.5
    slow = jax.random.uniform(jax.random.fold_in(key, 1), (4, 1)) < share_slow
    fast_len = KN_DEV / 8.0 + (KN_DEV / 5.0 - KN_DEV / 8.0) * jax.random.uniform(jax.random.fold_in(key, 2), (4, 1))
    slow_rate = math.log(10.0) * jax.random.uniform(jax.random.fold_in(key, 3), (4, 1), jnp.float32, 0.03, 0.15) / ATTITUDE_KNOTS
    base_rate = jnp.where(slow, slow_rate, 1.0 / fast_len)
    rough = jax.random.uniform(jax.random.fold_in(key, 4), (4, ATTITUDE_KNOTS), jnp.float32, 0.5, 1.5)
    device_scale = jnp.repeat(jax.random.uniform(jax.random.fold_in(key, 5), (4, RANGES), jnp.float32, 1.0, 2.5), KN_DEV, axis=1)
    rates = base_rate * rough * device_scale
    multiplier = jax.random.uniform(jax.random.fold_in(key, 6), (4, ATTITUDE_KNOTS), jnp.float32, 0.5, 0.8)
    sudden_jump = jax.random.uniform(jax.random.fold_in(key, 7), (4, ATTITUDE_KNOTS)) < 3.0 / ATTITUDE_KNOTS
    retained_entries = jnp.exp(-rates)
    return jnp.where(sudden_jump, retained_entries * multiplier, retained_entries).astype(jnp.float32)


def draw_calib_partials(key, part):
    base_scale = math.sqrt(CAL / OBS_TOTAL) / 4.64
    spread = jnp.exp(math.log(10.0) * jax.random.uniform(jax.random.fold_in(key, 1), (1, OBS_TOTAL)))
    values = jnp.clip(jax.random.normal(jax.random.fold_in(key, 2), (3, OBS_TOTAL)), -5.0, 5.0)
    return (values * spread * base_scale).astype(jnp.float32)


def with_ends(values, stream_key, least, top_value):
    longest = values.shape.index(max(values.shape))
    spots = []
    for shift in (0, 1):
        where = [jax.random.randint(jax.random.fold_in(stream_key, axis), (), 0, length) for axis, length in enumerate(values.shape)]
        where[longest] = (where[longest] + shift) % values.shape[longest]
        spots.append(tuple(where))
    return values.at[spots[0]].set(least).at[spots[1]].set(top_value)


def levels(own_key, extent, split, low, largest):
    level, own = 1.0, jax.random.fold_in(own_key, 6)
    for axis_at, parts in split:
        draws = jnp.exp(jax.random.uniform(jax.random.fold_in(own, axis_at), (parts,), jnp.float32, low / len(split), largest / len(split)))
        level = level * jnp.repeat(draws, extent[axis_at] // parts).reshape([-1 if axis == axis_at else 1 for axis in range(len(extent))])
    return level


def scatter_about(stream_key, shape, width, reach, split=(), kind=jnp.bfloat16):
    loudness = levels(stream_key, shape, split, -0.22, 0.18) if split else 1.0
    drawn = jax.random.normal(stream_key, shape, jnp.float32) * width * loudness
    return jnp.minimum(jnp.maximum(drawn, -reach), reach).astype(kind)


def setup_inputs(seed: int = 0) -> dict:
    arg_keys = jax.random.split(jax.random.key(seed), 13)
    prefit_resid = scatter_about(arg_keys[0], (OBS_TOTAL,), 1.0, 6.0, ((0, 32),), jnp.float32)
    source_partials = scatter_about(arg_keys[1], (5, OBS_TOTAL), 1.0, 6.0, ((1, 32),), jnp.float32)
    attitude_partials = scatter_about(arg_keys[2], (4, OBS_TOTAL), (OBS_TOTAL // ATTITUDE_KNOTS) ** -0.5, 0.25, ((1, 32),), jnp.float32)
    spline_position = jnp.clip(1.0 * jax.random.uniform(arg_keys[3], (OBS_TOTAL,), jnp.float32) ** levels(arg_keys[3], (OBS_TOTAL,), ((0, 32),), -0.2, 0.2), 0.0, 1.0)
    calib_partials = draw_calib_partials(jax.random.fold_in(arg_keys[12], 71), 0)
    obs_source = with_ends(jax.random.randint(arg_keys[5], (OBS_TOTAL,), 0, SRC_BLK), jax.random.fold_in(arg_keys[5], 1), 0, SRC_BLK - 1).astype(jnp.int32)
    block_count = draw_block_count(jax.random.fold_in(arg_keys[12], 71), 0)
    obs_range = draw_obs_range(jax.random.fold_in(arg_keys[12], 71), 0)
    obs_knot = with_ends(jax.random.randint(arg_keys[8], (OBS_TOTAL,), 0, KN_DEV), jax.random.fold_in(arg_keys[8], 1), 0, KN_DEV - 1).astype(jnp.int32)
    obs_unit = with_ends(jax.random.randint(arg_keys[9], (OBS_TOTAL,), 0, CAL), jax.random.fold_in(arg_keys[9], 1), 0, CAL - 1).astype(jnp.int32)
    given_inverse = draw_given_inverse(jax.random.fold_in(arg_keys[12], 71), 0)
    knot_decay = draw_knot_decay(jax.random.fold_in(arg_keys[12], 71), 0)
    return {"prefit_resid": prefit_resid, "source_partials": source_partials, "attitude_partials": attitude_partials, "spline_position": spline_position, "calib_partials": calib_partials, "obs_source": obs_source, "block_count": block_count, "obs_range": obs_range, "obs_knot": obs_knot, "obs_unit": obs_unit, "given_inverse": given_inverse, "knot_decay": knot_decay}


source_pairs = [(left_at, right_at) for left_at in range(5) for right_at in range(left_at, 5)]
calib_pairs = [(left_at, right_at) for left_at in range(3) for right_at in range(left_at, 3)]

def spline(position):
    remain = 1.0 - position
    square_pos = position * position
    cube_pos = square_pos * position
    return jnp.stack([remain * remain * remain / 6.0, (3.0 * cube_pos - 6.0 * square_pos + 4.0) / 6.0, (-3.0 * cube_pos + 3.0 * square_pos + 3.0 * position + 1.0) / 6.0, cube_pos / 6.0])

def symmetric(values, pair_list, order_size):
    matrix = [[None] * order_size for index_lookup in range(order_size)]
    for slot_at, (left_at, right_at) in enumerate(pair_list):
        diag_add = 1.0 if left_at == right_at else 0.0
        entry_val = values[slot_at] + diag_add
        matrix[left_at][right_at] = entry_val
        matrix[right_at][left_at] = entry_val
    return matrix

def spd_solve(matrix, target):
    order_size = len(target)
    lower_tri = [[None] * order_size for index_lookup in range(order_size)]
    for column in range(order_size):
        pivot_sq = matrix[column][column]
        for before in range(column):
            pivot_sq = pivot_sq - lower_tri[column][before] * lower_tri[column][before]
        pivot_root = jnp.sqrt(pivot_sq)
        lower_tri[column][column] = pivot_root
        for row_at in range(column + 1, order_size):
            entry_val = matrix[row_at][column]
            for before in range(column):
                entry_val = entry_val - lower_tri[row_at][before] * lower_tri[column][before]
            lower_tri[row_at][column] = entry_val / pivot_root
    forward_sol = []
    for row_at in range(order_size):
        running = target[row_at]
        for before in range(row_at):
            running = running - lower_tri[row_at][before] * forward_sol[before]
        forward_sol.append(running / lower_tri[row_at][row_at])
    answer = [None] * order_size
    for row_at in reversed(range(order_size)):
        running = forward_sol[row_at]
        for before in range(row_at + 1, order_size):
            running = running - lower_tri[before][row_at] * answer[before]
        answer[row_at] = running / lower_tri[row_at][row_at]
    return answer

def reference(prefit_resid, source_partials, attitude_partials, spline_position, calib_partials, obs_source, block_count, obs_range, obs_knot, obs_unit, given_inverse, knot_decay):
    count_obs = prefit_resid.shape[0]
    slot_index = jnp.arange(count_obs, dtype=jnp.int32)
    block_index = slot_index // SLOT_BLK
    valid_mask = (slot_index % SLOT_BLK < block_count[block_index]).astype(jnp.float32)
    source_index = block_index * SRC_BLK + obs_source
    term_list = [source_partials[left_at] * source_partials[right_at] * valid_mask for left_at, right_at in source_pairs]
    term_list = term_list + [source_partials[param_at] * prefit_resid * valid_mask for param_at in range(5)]
    block_sums = [jax.ops.segment_sum(term_at, source_index, num_segments=SOURCES) for term_at in term_list]
    matrix = symmetric(block_sums[:15], source_pairs, 5)
    source_update = jnp.stack(spd_solve(matrix, block_sums[15:]))
    update_at_obs = source_update[:, source_index]
    resid_after = valid_mask * (prefit_resid - lax.optimization_barrier(jnp.sum(source_partials * update_at_obs, axis=0)))
    interval = obs_range * KN_DEV + obs_knot
    weights = spline(spline_position)
    columns = []
    for comp_at in range(4):
        line_sum = jnp.zeros((ATTITUDE_KNOTS + 3,), jnp.float32)
        for shift_at in range(4):
            line_sum = line_sum + jax.ops.segment_sum(weights[shift_at] * attitude_partials[comp_at] * resid_after, interval + shift_at, num_segments=ATTITUDE_KNOTS + 3)
        columns.append(line_sum[:ATTITUDE_KNOTS])
    att_rhs = jnp.stack(columns)
    span_rhs = att_rhs.reshape(4, RANGES, KN_DEV).transpose(1, 0, 2).reshape(RANGES, 4 * KN_DEV)
    solution_vector = jnp.einsum('rij,rj->ri', given_inverse, span_rhs, precision=lax.Precision.HIGHEST)
    solution_vector = solution_vector.reshape(RANGES, 4, KN_DEV).transpose(1, 0, 2).reshape(4, ATTITUDE_KNOTS)
    knot_gain = jnp.sqrt(1.0 - knot_decay * knot_decay)

    def advance(carried, inputs):
        rate_now, gain_now, value_now = inputs
        carried = rate_now * carried + gain_now * value_now
        return (carried, carried)
    final_state, history = lax.scan(advance, jnp.zeros((4,), jnp.float32), (knot_decay.T, knot_gain.T, solution_vector.T))
    attitude_update = history.T
    masked_cal = valid_mask * calib_partials
    cal_terms = [masked_cal[left_at] * masked_cal[right_at] for left_at, right_at in calib_pairs]
    cal_terms = cal_terms + [masked_cal[param_at] * resid_after for param_at in range(3)]
    cal_sums = [jax.ops.segment_sum(term_at, obs_unit, num_segments=CAL) for term_at in cal_terms]
    cal_matrix = symmetric(cal_sums[:6], calib_pairs, 3)
    cal_update = jnp.stack(spd_solve(cal_matrix, cal_sums[6:]))
    return (source_update, attitude_update, cal_update)
```

```python
import functools

import jax
import jax.numpy as jnp
from jax import lax
from jax.experimental import pallas as pl
from jax.experimental.pallas import tpu as pltpu
from jax.sharding import PartitionSpec as P

SRC_BLK = 128
SLOT_BLK = 640
CAL = 2016
SPLIT = 4
ROWS = 24
NT = (((1,), (1,)), ((), ()))
F32 = jnp.float32
BF16 = jnp.bfloat16


def source_row(i, j):
    d = i - j
    return d * 8 + i if d <= 4 else 3 * 8 + j


def ldl_solve(matrix, target):
    n = len(target)
    low = [[None] * n for _ in range(n)]
    inv = [None] * n
    for c in range(n):
        scaled = [low[c][b][1] for b in range(c)]
        d = matrix(c, c) + 1.0
        for b in range(c):
            d = d - scaled[b] * low[c][b][0]
        inv[c] = 1.0 / d
        for r in range(c + 1, n):
            v = matrix(r, c)
            for b in range(c):
                v = v - low[r][b][1] * low[c][b][0]
            low[r][c] = (v * inv[c], v)
    z = []
    for r in range(n):
        v = target[r]
        for b in range(r):
            v = v - low[r][b][0] * z[b]
        z.append(v)
    x = [None] * n
    for r in reversed(range(n)):
        v = z[r] * inv[r]
        for b in range(r + 1, n):
            v = v - low[b][r][0] * x[b]
        x[r] = v
    return x


def split3(v):
    hi = v.astype(BF16).astype(F32)
    rest = v - hi
    mid = rest.astype(BF16).astype(F32)
    return hi, mid, rest - mid


def local_kernel(
    blocks, ranges, narrow,
    count_ref, resid_ref, sp_ref, att_ref, pos_ref, cal_ref, src_ref, rng_ref, knot_ref, unit_ref,
    update_ref, send_ref,
    e_ref, s_ref, x_ref, iota_ref, acc_att, acc_cal,
):
    iota_ref[...] = lax.broadcasted_iota(jnp.int32, (256, 128), 0).astype(F32).astype(BF16)
    slot = lax.broadcasted_iota(jnp.int32, (1, SLOT_BLK), 1)

    def normals(b, carry):
        at = pl.multiple_of(b * SLOT_BLK, 128)
        cols = pl.ds(at, SLOT_BLK)
        e = jnp.concatenate(
            [sp_ref[:, cols], resid_ref[:, cols], jnp.zeros((2, SLOT_BLK), F32)], axis=0
        )
        live = jnp.broadcast_to(slot < count_ref[b], (8, SLOT_BLK))
        e = jnp.where(live, e, 0.0)
        e_ref[:, cols] = e
        terms = jnp.concatenate(
            [e * e] + [e * pltpu.roll(e, d, axis=0) for d in range(1, 5)], axis=0
        )
        left = jnp.concatenate(split3(terms), axis=0).astype(BF16)
        src = src_ref[:, cols].astype(F32).astype(BF16)
        grid = jnp.concatenate([iota_ref[0:SRC_BLK, :]] * (SLOT_BLK // 128), axis=1)
        hot = jnp.where(grid == src, jnp.ones((), BF16), jnp.zeros((), BF16))
        sums = lax.dot_general(left, hot, NT, preferred_element_type=F32)
        s_ref[pl.ds(b, 40, stride=blocks), :] = sums[0:40] + sums[40:80] + sums[80:120]
        return carry

    lax.fori_loop(0, blocks, normals, 0, unroll=2)

    group = 16
    for g in range(0, blocks, group):
        def entry(i, j, g=g):
            row = source_row(i, j) * blocks + g
            return s_ref[row:row + group, :]

        x = ldl_solve(entry, [entry(5, j) for j in range(5)])
        for p in range(5):
            x_ref[pl.ds(g * 8 + p, group, stride=8), :] = x[p]
        x_ref[pl.ds(g * 8 + 5, group, stride=8), :] = jnp.full((group, 128), -1.0, F32)
        for p in (6, 7):
            x_ref[pl.ds(g * 8 + p, group, stride=8), :] = jnp.zeros((group, 128), F32)

    acc_att[...] = jnp.zeros_like(acc_att)
    acc_cal[...] = jnp.zeros_like(acc_cal)
    wide_slots = 2 * SLOT_BLK
    sub8 = lax.broadcasted_iota(jnp.int32, (8, wide_slots), 0)
    first = sub8 < 4
    per_row = 2 * (CAL // (narrow * SPLIT))

    def horner(u, low, high):
        c = [jnp.where(first, low[i], high[i]) for i in range(4)]
        return c[0] + u * (c[1] + u * (c[2] + u * c[3]))

    def rest(t, carry):
        at = pl.multiple_of(t * wide_slots, 128)
        cols = pl.ds(at, wide_slots)
        src = src_ref[:, cols]
        gathered = []
        for half in range(2):
            b = t * 2 + half
            table = x_ref[pl.ds(pl.multiple_of(b * 8, 8), 8), :]
            update_ref[:, pl.ds(pl.multiple_of(b * 128, 128), 128)] = table[0:5, :]
            for q in range(SLOT_BLK // 128):
                lo = half * SLOT_BLK + q * 128
                ids = jnp.broadcast_to(src[:, lo:lo + 128], (8, 128))
                gathered.append(jnp.take_along_axis(table, ids, axis=1, mode="promise_in_bounds"))
        prod = e_ref[:, cols] * jnp.concatenate(gathered, axis=1)
        prod = prod + pltpu.roll(prod, 4, axis=0)
        prod = prod + pltpu.roll(prod, 2, axis=0)
        prod = prod + pltpu.roll(prod, 1, axis=0)
        after = -prod

        u = jnp.broadcast_to(pos_ref[:, cols], (8, wide_slots))
        sixth = 1.0 / 6.0
        w01 = horner(u, (sixth, -0.5, 0.5, -sixth), (4.0 / 6.0, 0.0, -1.0, 0.5))
        w23 = horner(u, (sixth, 0.5, 0.5, -0.5), (0.0, 0.0, 0.0, sixth))
        att = att_ref[:, cols]
        scaled = jnp.concatenate([att, att], axis=0) * after
        terms = jnp.concatenate([scaled * w01, scaled * w23], axis=0)
        hi = terms.astype(BF16)
        pieces = jnp.concatenate([hi, (terms - hi.astype(F32)).astype(BF16)], axis=0)
        rng = jnp.broadcast_to(rng_ref[:, cols].astype(F32).astype(BF16), (32, wide_slots))
        zero = jnp.zeros((), BF16)
        one = jnp.ones((), BF16)
        left = jnp.concatenate(
            [jnp.where(rng == jnp.asarray(r, BF16), pieces, zero) for r in range(ranges)], axis=0
        )
        grid = jnp.concatenate([iota_ref[...]] * (wide_slots // 128), axis=1)
        knot = knot_ref[:, cols].astype(F32).astype(BF16)
        hot = jnp.where(grid == knot, one, zero)
        acc_att[...] += lax.dot_general(left, hot, NT, preferred_element_type=F32)

        slot2 = lax.broadcasted_iota(jnp.int32, (1, SLOT_BLK), 1)
        live = jnp.concatenate(
            [slot2 < count_ref[2 * t], slot2 < count_ref[2 * t + 1]], axis=1
        )
        cal = jnp.where(live, cal_ref[:, cols], 0.0)
        four = jnp.concatenate([cal, after[0:1, :]], axis=0)
        f = jnp.concatenate([four, four], axis=0)
        near = f * jnp.where(first, f, pltpu.roll(f, 1, axis=0))
        far = f * pltpu.roll(f, 2, axis=0)
        far_hi, far_mid, far_lo = split3(far)
        far = jnp.where(sub8 < 2, far_hi, jnp.where(first, far_mid, jnp.where(sub8 < 6, far_lo, 0.0)))
        pieces = jnp.concatenate(list(split3(near)) + [far], axis=0).astype(BF16)
        unit = unit_ref[:, cols]
        upper = (unit * ((1 << 22) // per_row + 1)) >> 22
        place = unit - upper * per_row
        place = place + jnp.where(place >= per_row // 2, 128 - per_row // 2, 0)
        upper = jnp.broadcast_to(upper.astype(F32).astype(BF16), (32, wide_slots))
        left = jnp.concatenate(
            [jnp.where(upper == jnp.asarray(r, BF16), pieces, zero) for r in range(narrow * SPLIT // 2)],
            axis=0,
        )
        hot = jnp.where(grid == place.astype(F32).astype(BF16), one, zero)
        acc_cal[...] += lax.dot_general(left, hot, NT, preferred_element_type=F32)
        return carry

    lax.fori_loop(0, blocks // 2, rest, 0)

    lane = lax.broadcasted_iota(jnp.int32, (4, 256), 1)
    cal_pieces = []
    for piece in range(narrow * SPLIT):
        top, half = piece // 2, (piece % 2) * 128
        part = acc_cal[top * 32:(top + 1) * 32, half:half + 128]
        near = part[0:8] + part[8:16] + part[16:24]
        far = part[24:26] + part[26:28] + part[28:30]
        cal_pieces.append((near, far))
    before = None
    for r in range(ranges):
        part = acc_att[r * 32:r * 32 + 16, :] + acc_att[r * 32 + 16:r * 32 + 32, :]
        rolled = [part[0:4]] + [pltpu.roll(part[4 * k:4 * k + 4], k, axis=1) for k in range(1, 4)]
        total = rolled[0]
        for k in range(1, 4):
            wrapped = jnp.zeros((4, 256), F32) if before is None else before[k]
            total = total + jnp.where(lane >= k, rolled[k], wrapped)
        before = rolled
        for n in range(narrow):
            d = r * narrow + n
            near, far = cal_pieces[n * SPLIT + r % SPLIT]
            send_ref[d, 0:4, :] = total[:, 0:128]
            send_ref[d, 4:8, :] = total[:, 128:256]
            send_ref[d, 8:16, :] = near
            send_ref[d, 16:18, :] = far
            send_ref[d, 18:24, :] = jnp.zeros((6, 128), F32)


def exchange_kernel(
    wide, narrow,
    send_ref, inverse_ref, decay_ref,
    att_out, cal_out,
    recv, g_ref, carry_buf, cal_buf,
    g_sem, send_sem, recv_sem, carry_send, carry_recv, cal_send, cal_recv,
):
    count = wide * narrow
    w = lax.axis_index("wide")
    n = lax.axis_index("narrow")
    me = w * narrow + n
    mesh_id = pl.DeviceIdType.MESH
    load = pltpu.make_async_copy(inverse_ref.at[0], g_ref, g_sem)
    load.start()

    barrier = pltpu.get_barrier_semaphore()

    def greet(i, c):
        d = lax.rem(me + i, count)
        pl.semaphore_signal(
            barrier, inc=1, device_id=(d // narrow, lax.rem(d, narrow)), device_id_type=mesh_id
        )
        return c

    lax.fori_loop(1, count, greet, 0)
    pl.semaphore_wait(barrier, count - 1)

    def block_copy(i, slot):
        d = lax.rem(me + i, count)
        return pltpu.make_async_remote_copy(
            src_ref=send_ref.at[d],
            dst_ref=recv.at[slot],
            send_sem=send_sem.at[i],
            recv_sem=recv_sem.at[slot],
            device_id=(d // narrow, lax.rem(d, narrow)),
            device_id_type=mesh_id,
        )

    def launch(i, c):
        block_copy(i, me).start()
        return c

    lax.fori_loop(1, count, launch, 0)

    def collect(i, total):
        s = lax.rem(me + count - i, count)
        block_copy(i, s).wait_recv()
        return total + recv[s]

    total = lax.fori_loop(1, count, collect, send_ref[me])

    near, far = total[8:16], total[16:18]
    pair = {
        (0, 0): near[0:1], (1, 1): near[1:2], (2, 2): near[2:3],
        (1, 0): near[5:6], (2, 1): near[6:7], (2, 0): far[0:1],
    }
    x = ldl_solve(lambda i, j: pair[(i, j)], [near[4:5], far[1:2], near[7:8]])
    base = (w // SPLIT) * SPLIT
    mine = lax.rem(w, SPLIT)
    cal_buf[mine] = jnp.concatenate(x + [jnp.zeros((5, 128), F32)], axis=0)

    def cal_copy(i, slot):
        to = lax.rem(mine + i, SPLIT)
        return pltpu.make_async_remote_copy(
            src_ref=cal_buf.at[mine],
            dst_ref=cal_buf.at[slot],
            send_sem=cal_send.at[i],
            recv_sem=cal_recv.at[slot],
            device_id=(base + to, n),
            device_id_type=mesh_id,
        )

    for i in range(1, SPLIT):
        cal_copy(i, mine).start()

    columns = total[0:8].T
    load.wait()
    y = jnp.zeros((8, 1024), F32)
    for r in range(8):
        at = (r % 4) * 256 + (r // 4) * 128
        prod = columns[:, r:r + 1] * g_ref[at:at + 128, :]
        for j in range(16):
            y = y + prod[j * 8:(j + 1) * 8]
    y = jnp.sum(y, axis=0, keepdims=True)
    value = jnp.concatenate([y[:, c * 256:(c + 1) * 256] for c in range(4)], axis=0)
    mul = decay_ref[...]
    add = jnp.sqrt(1.0 - mul * mul) * value
    lane = lax.broadcasted_iota(jnp.int32, (4, 256), 1)
    step = 1
    while step < 256:
        inside = lane >= step
        add = add + mul * jnp.where(inside, pltpu.roll(add, step, axis=1), 0.0)
        mul = mul * jnp.where(inside, pltpu.roll(mul, step, axis=1), 1.0)
        step *= 2
    carry_buf[w] = jnp.concatenate(
        [jnp.broadcast_to(mul[:, 255:256], (4, 128)), jnp.broadcast_to(add[:, 255:256], (4, 128))],
        axis=0,
    )

    def carry_copy(i, slot):
        to = lax.rem(w + i, wide)
        return pltpu.make_async_remote_copy(
            src_ref=carry_buf.at[w],
            dst_ref=carry_buf.at[slot],
            send_sem=carry_send.at[i],
            recv_sem=carry_recv.at[slot],
            device_id=(to, n),
            device_id_type=mesh_id,
        )

    for i in range(1, wide):
        carry_copy(i, w).start()
    for i in range(1, SPLIT):
        cal_copy(i, lax.rem(mine + SPLIT - i, SPLIT)).wait_recv()
    for j in range(SPLIT):
        cal_out[j] = cal_buf[j]
    for i in range(1, wide):
        carry_copy(i, lax.rem(w + wide - i, wide)).wait_recv()
    state = jnp.zeros((4, 128), F32)
    for p in range(wide):
        piece = carry_buf[p]
        state = jnp.where(p < w, piece[0:4] * state + piece[4:8], state)
    att_out[...] = add + mul * jnp.concatenate([state, state], axis=1)

    def drain(i, c):
        block_copy(i, me).wait_send()
        return c

    lax.fori_loop(1, count, drain, 0)
    for i in range(1, SPLIT):
        cal_copy(i, mine).wait_send()
    for i in range(1, wide):
        carry_copy(i, w).wait_send()


def on_device(
    prefit_resid, source_partials, attitude_partials, spline_position, calib_partials, obs_source,
    block_count, obs_range, obs_knot, obs_unit, given_inverse, knot_decay,
):
    wide = lax.axis_size("wide")
    narrow = lax.axis_size("narrow")
    blocks = block_count.shape[0]
    slots = prefit_resid.shape[0]
    count = wide * narrow
    vmem = pl.BlockSpec(memory_space=pltpu.VMEM)
    row = lambda v: v.reshape(1, slots)
    source_update, send = pl.pallas_call(
        functools.partial(local_kernel, blocks, wide, narrow),
        out_shape=(
            jax.ShapeDtypeStruct((5, blocks * SRC_BLK), F32),
            jax.ShapeDtypeStruct((count, ROWS, 128), F32),
        ),
        in_specs=[pl.BlockSpec(memory_space=pltpu.SMEM)] + [vmem] * 9,
        out_specs=(vmem, vmem),
        scratch_shapes=[
            pltpu.VMEM((8, slots), F32),
            pltpu.VMEM((40 * blocks, 128), F32),
            pltpu.VMEM((8 * blocks, 128), F32),
            pltpu.VMEM((256, 128), BF16),
            pltpu.VMEM((wide * 32, 256), F32),
            pltpu.VMEM((narrow * SPLIT // 2 * 32, 256), F32),
        ],
        compiler_params=pltpu.CompilerParams(vmem_limit_bytes=56 * 1024 * 1024),
        name="local_sums",
    )(
        block_count, row(prefit_resid), source_partials, attitude_partials, row(spline_position),
        calib_partials, row(obs_source), row(obs_range), row(obs_knot), row(obs_unit),
    )
    dma = pltpu.SemaphoreType.DMA
    attitude_update, cal = pl.pallas_call(
        functools.partial(exchange_kernel, wide, narrow),
        out_shape=(
            jax.ShapeDtypeStruct(knot_decay.shape, F32),
            jax.ShapeDtypeStruct((SPLIT, 8, 128), F32),
        ),
        in_specs=[vmem, pl.BlockSpec(memory_space=pl.ANY), vmem],
        out_specs=(vmem, vmem),
        scratch_shapes=[
            pltpu.VMEM((count, ROWS, 128), F32),
            pltpu.VMEM(given_inverse.shape[1:], F32),
            pltpu.VMEM((wide, 8, 128), F32),
            pltpu.VMEM((SPLIT, 8, 128), F32),
            dma,
            dma((count,)), dma((count,)),
            dma((wide,)), dma((wide,)),
            dma((SPLIT,)), dma((SPLIT,)),
        ],
        compiler_params=pltpu.CompilerParams(
            collective_id=0, has_side_effects=True, vmem_limit_bytes=32 * 1024 * 1024
        ),
        name="exchange",
    )(send, given_inverse, knot_decay)
    per = CAL // (narrow * SPLIT)
    cal_update = cal[:, 0:3, 0:per].transpose(1, 0, 2).reshape(3, SPLIT * per)
    return (source_update, attitude_update, cal_update)


def solution(mesh):
    both = P(("wide", "narrow"))
    rows = P(None, ("wide", "narrow"))
    placed = (
        both, rows, rows, both, rows, both, both, both, both, both, P("wide", None, None), P(None, "wide"),
    )
    return jax.shard_map(
        on_device,
        mesh=mesh,
        in_specs=placed,
        out_specs=(rows, P(None, "wide"), P(None, "narrow")),
        check_vma=False,
    )
```

```python
import functools

import jax
import jax.numpy as jnp
from jax import lax
from jax.experimental import pallas as pl
from jax.experimental.pallas import tpu as pltpu
from jax.sharding import PartitionSpec as P

SRC_BLK = 128
SLOT_BLK = 640
CAL = 2016
SPLIT = 8
NT = (((1,), (1,)), ((), ()))
F32 = jnp.float32
BF16 = jnp.bfloat16


def source_row(i, j):
    d = i - j
    return d * 8 + i if d <= 4 else 3 * 8 + j


def ldl_solve(matrix, target):
    n = len(target)
    low = [[None] * n for _ in range(n)]
    inv = [None] * n
    for c in range(n):
        scaled = [low[c][b][1] for b in range(c)]
        d = matrix(c, c) + 1.0
        for b in range(c):
            d = d - scaled[b] * low[c][b][0]
        inv[c] = 1.0 / d
        for r in range(c + 1, n):
            v = matrix(r, c)
            for b in range(c):
                v = v - low[r][b][1] * low[c][b][0]
            low[r][c] = (v * inv[c], v)
    z = []
    for r in range(n):
        v = target[r]
        for b in range(r):
            v = v - low[r][b][0] * z[b]
        z.append(v)
    x = [None] * n
    for r in reversed(range(n)):
        v = z[r] * inv[r]
        for b in range(r + 1, n):
            v = v - low[b][r][0] * x[b]
        x[r] = v
    return x


def split3(v):
    hi = v.astype(BF16).astype(F32)
    rest = v - hi
    mid = rest.astype(BF16).astype(F32)
    return hi, mid, rest - mid


def local_kernel(
    blocks, ranges, narrow,
    count_ref, resid_hbm, sp_hbm, src_hbm, att_hbm, pos_hbm, cal_hbm, rng_hbm, knot_hbm, unit_hbm,
    update_ref, send_ref,
    e_ref, s_ref, x_ref, iota_ref, acc_att, acc_cal,
    resid_ref, sp_ref, src_ref, att_ref, pos_ref, cal_ref, rng_ref, knot_ref, unit_ref, sems,
):
    moves = [
        (resid_hbm, resid_ref), (sp_hbm, sp_ref), (src_hbm, src_ref),
        (att_hbm, att_ref), (pos_hbm, pos_ref), (cal_hbm, cal_ref),
        (rng_hbm, rng_ref), (knot_hbm, knot_ref), (unit_hbm, unit_ref),
    ]
    loads = [pltpu.make_async_copy(a, b, sems.at[k]) for k, (a, b) in enumerate(moves)]
    for load in loads:
        load.start()
    iota_ref[...] = lax.broadcasted_iota(jnp.int32, (256, 128), 0).astype(F32).astype(BF16)
    slot = lax.broadcasted_iota(jnp.int32, (1, SLOT_BLK), 1)
    for load in loads[0:3]:
        load.wait()

    def normals(b, carry):
        at = pl.multiple_of(b * SLOT_BLK, 128)
        cols = pl.ds(at, SLOT_BLK)
        e = jnp.concatenate(
            [sp_ref[:, cols], resid_ref[:, cols], jnp.zeros((2, SLOT_BLK), F32)], axis=0
        )
        live = jnp.broadcast_to(slot < count_ref[b], (8, SLOT_BLK))
        e = jnp.where(live, e, 0.0)
        e_ref[:, cols] = e
        terms = jnp.concatenate(
            [e * e] + [e * pltpu.roll(e, d, axis=0) for d in range(1, 5)], axis=0
        )
        left = jnp.concatenate(split3(terms), axis=0).astype(BF16)
        src = src_ref[:, cols].astype(F32).astype(BF16)
        grid = jnp.concatenate([iota_ref[0:SRC_BLK, :]] * (SLOT_BLK // 128), axis=1)
        hot = jnp.where(grid == src, jnp.ones((), BF16), jnp.zeros((), BF16))
        sums = lax.dot_general(left, hot, NT, preferred_element_type=F32)
        s_ref[pl.ds(b, 40, stride=blocks), :] = sums[0:40] + sums[40:80] + sums[80:120]
        return carry

    lax.fori_loop(0, blocks, normals, 0, unroll=4)

    group = 16
    for g in range(0, blocks, group):
        def entry(i, j, g=g):
            row = source_row(i, j) * blocks + g
            return s_ref[row:row + group, :]

        x = ldl_solve(entry, [entry(5, j) for j in range(5)])
        for p in range(5):
            x_ref[pl.ds(g * 8 + p, group, stride=8), :] = x[p]
        x_ref[pl.ds(g * 8 + 5, group, stride=8), :] = jnp.full((group, 128), -1.0, F32)
        for p in (6, 7):
            x_ref[pl.ds(g * 8 + p, group, stride=8), :] = jnp.zeros((group, 128), F32)

    for load in loads[3:9]:
        load.wait()
    acc_att[...] = jnp.zeros_like(acc_att)
    acc_cal[...] = jnp.zeros_like(acc_cal)
    wide_slots = 2 * SLOT_BLK
    sub8 = lax.broadcasted_iota(jnp.int32, (8, wide_slots), 0)
    first = sub8 < 4
    per = CAL // (narrow * SPLIT)
    per_row = 4 * per

    def horner(u, low, high):
        c = [jnp.where(first, low[i], high[i]) for i in range(4)]
        return c[0] + u * (c[1] + u * (c[2] + u * c[3]))

    def rest(t, carry):
        at = pl.multiple_of(t * wide_slots, 128)
        cols = pl.ds(at, wide_slots)
        src = src_ref[:, cols]
        gathered = []
        for half in range(2):
            b = t * 2 + half
            table = x_ref[pl.ds(pl.multiple_of(b * 8, 8), 8), :]
            update_ref[:, pl.ds(pl.multiple_of(b * 128, 128), 128)] = table[0:5, :]
            for q in range(SLOT_BLK // 128):
                lo = half * SLOT_BLK + q * 128
                ids = jnp.broadcast_to(src[:, lo:lo + 128], (8, 128))
                gathered.append(jnp.take_along_axis(table, ids, axis=1, mode="promise_in_bounds"))
        prod = e_ref[:, cols] * jnp.concatenate(gathered, axis=1)
        prod = prod + pltpu.roll(prod, 4, axis=0)
        prod = prod + pltpu.roll(prod, 2, axis=0)
        prod = prod + pltpu.roll(prod, 1, axis=0)
        after = -prod

        u = jnp.broadcast_to(pos_ref[:, cols], (8, wide_slots))
        sixth = 1.0 / 6.0
        w01 = horner(u, (sixth, -0.5, 0.5, -sixth), (4.0 / 6.0, 0.0, -1.0, 0.5))
        w23 = horner(u, (sixth, 0.5, 0.5, -0.5), (0.0, 0.0, 0.0, sixth))
        att = att_ref[:, cols]
        scaled = jnp.concatenate([att, att], axis=0) * after
        terms = jnp.concatenate([scaled * w01, scaled * w23], axis=0)
        hi = terms.astype(BF16)
        pieces = jnp.concatenate([hi, (terms - hi.astype(F32)).astype(BF16)], axis=0)
        rng = jnp.broadcast_to(rng_ref[:, cols].astype(F32).astype(BF16), (16, wide_slots))
        zero = jnp.zeros((), BF16)
        one = jnp.ones((), BF16)

        def masked(ids, r, parts):
            here = ids == jnp.asarray(r, BF16)
            return [jnp.where(here, parts[k:k + 16], zero) for k in (0, 16)]

        left = jnp.concatenate(
            [v for r in range(ranges) for v in masked(rng, r, pieces)], axis=0
        )
        grid = jnp.concatenate([iota_ref[...]] * (wide_slots // 128), axis=1)
        knot = knot_ref[:, cols].astype(F32).astype(BF16)
        hot = jnp.where(grid == knot, one, zero)
        acc_att[...] += lax.dot_general(left, hot, NT, preferred_element_type=F32)

        slot2 = lax.broadcasted_iota(jnp.int32, (1, SLOT_BLK), 1)
        live = jnp.concatenate(
            [slot2 < count_ref[2 * t], slot2 < count_ref[2 * t + 1]], axis=1
        )
        cal = jnp.where(live, cal_ref[:, cols], 0.0)
        four = jnp.concatenate([cal, after[0:1, :]], axis=0)
        f = jnp.concatenate([four, four], axis=0)
        near = f * jnp.where(first, f, pltpu.roll(f, 1, axis=0))
        far = f * pltpu.roll(f, 2, axis=0)
        far_hi, far_mid, far_lo = split3(far)
        far = jnp.where(sub8 < 2, far_hi, jnp.where(first, far_mid, jnp.where(sub8 < 6, far_lo, 0.0)))
        pieces = jnp.concatenate(list(split3(near)) + [far], axis=0).astype(BF16)
        unit = unit_ref[:, cols]
        upper = (unit * ((1 << 22) // per_row + 1)) >> 22
        place = unit - upper * per_row
        late = [jnp.where(place >= q * per, 64 - per, 0) for q in range(1, 4)]
        place = place + (late[0] + late[1] + late[2])
        upper = jnp.broadcast_to(upper.astype(F32).astype(BF16), (16, wide_slots))
        left = jnp.concatenate(
            [v for r in range(narrow * 2) for v in masked(upper, r, pieces)],
            axis=0,
        )
        hot = jnp.where(grid == place.astype(F32).astype(BF16), one, zero)
        acc_cal[...] += lax.dot_general(left, hot, NT, preferred_element_type=F32)
        return carry

    lax.fori_loop(0, blocks // 2, rest, 0, unroll=2)

    lane = lax.broadcasted_iota(jnp.int32, (4, 256), 1)
    cal_pieces = []
    low = lax.broadcasted_iota(jnp.int32, (5, 128), 1) < 64
    for pair in range(narrow * SPLIT // 2):
        top, half = pair // 2, (pair % 2) * 128
        part = acc_cal[top * 32:(top + 1) * 32, half:half + 128]
        near = part[0:8] + part[8:16] + part[16:24]
        far = part[24:26] + part[26:28] + part[28:30]
        upper5 = near[0:5]
        lower5 = jnp.concatenate([near[5:8], far], axis=0)
        cal_pieces.append(jnp.where(low, upper5, pltpu.roll(lower5, 64, axis=1)))
        cal_pieces.append(jnp.where(low, pltpu.roll(upper5, 64, axis=1), lower5))
    before = None
    for r in range(ranges):
        part = acc_att[r * 32:r * 32 + 16, :] + acc_att[r * 32 + 16:r * 32 + 32, :]
        rolled = [part[0:4]] + [pltpu.roll(part[4 * k:4 * k + 4], k, axis=1) for k in range(1, 4)]
        total = rolled[0]
        for k in range(1, 4):
            wrapped = jnp.zeros((4, 256), F32) if before is None else before[k]
            total = total + jnp.where(lane >= k, rolled[k], wrapped)
        before = rolled
        for n in range(narrow):
            d = r * narrow + n
            send_ref[d, 0:1, :] = total[n:n + 1, 0:128]
            send_ref[d, 1:2, :] = total[n:n + 1, 128:256]
            send_ref[d, 2:7, :] = cal_pieces[n * SPLIT + r % SPLIT]
            send_ref[d, 7:8, :] = jnp.zeros((1, 128), F32)


def exchange_kernel(
    wide, narrow,
    send_ref, inverse_ref, decay_hbm,
    att_out, cal_out,
    recv, mine_buf, recv2, g_ref, decay_ref,
    send_sem, recv_sem, send_sem2, recv_sem2, local_sem,
):
    w = lax.axis_index("wide")
    n = lax.axis_index("narrow")
    me = w * narrow + n
    mesh_id = pl.DeviceIdType.MESH
    own = pl.ds(pl.multiple_of(n * 256, 256), 256)
    loads = [
        pltpu.make_async_copy(send_ref.at[me], recv.at[me], local_sem.at[0]),
        pltpu.make_async_copy(inverse_ref.at[0, own], g_ref, local_sem.at[1]),
        pltpu.make_async_copy(decay_hbm, decay_ref, local_sem.at[2]),
    ]
    for load in loads:
        load.start()

    def others(visit, carry, sign):
        ns = [lax.rem(n + (sign * dn) % narrow, narrow) for dn in range(narrow)]
        for dn in range(1, narrow):
            carry = visit(dn, w, ns[dn], carry)

        def row(dw, carry):
            to = lax.rem(w + wide + sign * dw, wide)
            for dn in range(narrow):
                carry = visit(dw * narrow + dn, to, ns[dn], carry)
            return carry

        return lax.fori_loop(1, wide, row, carry)

    barrier = pltpu.get_barrier_semaphore()

    def greet(i, tw, tn, c):
        pl.semaphore_signal(barrier, inc=1, device_id=(tw, tn), device_id_type=mesh_id)
        return c

    others(greet, 0, 1)
    pl.semaphore_wait(barrier, wide * narrow - 1)

    def first_copy(i, tw, tn, slot):
        return pltpu.make_async_remote_copy(
            src_ref=send_ref.at[tw * narrow + tn],
            dst_ref=recv.at[slot],
            send_sem=send_sem.at[i],
            recv_sem=recv_sem.at[slot],
            device_id=(tw, tn),
            device_id_type=mesh_id,
        )

    def first_start(i, tw, tn, c):
        first_copy(i, tw, tn, me).start()
        return c

    others(first_start, 0, 1)

    def collect(i, tw, tn, total):
        s = tw * narrow + tn
        first_copy(i, tw, tn, s).wait_recv()
        return total + recv[s]

    for load in loads:
        load.wait()
    total = others(collect, recv[me], -1)

    columns = total.T
    y = jnp.zeros((8, 1024), F32)
    for r in range(2):
        prod = columns[:, r:r + 1] * g_ref[r * 128:(r + 1) * 128, :]
        for j in range(16):
            y = y + prod[j * 8:(j + 1) * 8]
    y = jnp.sum(y, axis=0, keepdims=True)
    value = jnp.concatenate([y[:, c * 256:(c + 1) * 256] for c in range(4)], axis=0)
    mul = decay_ref[...]
    add = jnp.sqrt(1.0 - mul * mul) * value
    lane = lax.broadcasted_iota(jnp.int32, (4, 256), 1)
    step = 1
    while step < 256:
        inside = lane >= step
        add = add + mul * jnp.where(inside, pltpu.roll(add, step, axis=1), 0.0)
        mul = mul * jnp.where(inside, pltpu.roll(mul, step, axis=1), 1.0)
        step *= 2

    turned = pltpu.roll(total, 64, axis=1)
    q = [total[2 + j:3 + j] for j in range(5)] + [turned[2 + j:3 + j] for j in range(5)]
    pair = {(0, 0): q[0], (1, 1): q[1], (2, 2): q[2], (1, 0): q[5], (2, 1): q[6], (2, 0): q[8]}
    x = ldl_solve(lambda i, j: pair[(i, j)], [q[4], q[9], q[7]])
    x = pltpu.roll(jnp.concatenate(x + [jnp.zeros((5, 128), F32)], axis=0), 64, axis=1)
    last = jnp.concatenate(
        [jnp.broadcast_to(add[:, 255:256], (4, 128)), jnp.broadcast_to(mul[:, 255:256], (4, 128))],
        axis=0,
    )
    lane8 = lax.broadcasted_iota(jnp.int32, (8, 128), 1)
    far_msg = jnp.where(lane8 < 64, last, x)
    near_msg = jnp.concatenate([add[:, 0:128], add[:, 128:256]], axis=0)
    mine_buf[0] = near_msg
    mine_buf[1] = far_msg
    recv2[me] = near_msg

    def second_copy(i, tw, tn, slot):
        kind = 0 if isinstance(i, int) else 1
        return pltpu.make_async_remote_copy(
            src_ref=mine_buf.at[kind],
            dst_ref=recv2.at[slot],
            send_sem=send_sem2.at[i],
            recv_sem=recv_sem2.at[slot],
            device_id=(tw, tn),
            device_id_type=mesh_id,
        )

    def second_start(i, tw, tn, c):
        second_copy(i, tw, tn, me).start()
        return c

    others(second_start, 0, 1)

    def second_wait(i, tw, tn, c):
        second_copy(i, tw, tn, tw * narrow + tn).wait_recv()
        return c

    others(second_wait, 0, -1)

    base = (w // SPLIT) * SPLIT
    for j in range(SPLIT):
        cal_out[j] = jnp.where(base + j == w, far_msg, recv2[(base + j) * narrow + n])
    whole = recv2[w * narrow]
    for k in range(1, narrow):
        whole = whole + recv2[w * narrow + k]
    state = jnp.zeros((4, 128), F32)
    for p in range(wide):
        entry = recv2[p * narrow]
        part, rate = entry[0:4], entry[4:8]
        for k in range(1, narrow):
            part = part + recv2[p * narrow + k, 0:4, :]
        state = jnp.where(p < w, rate * state + part, state)
    entering = jnp.broadcast_to(state[:, 0:1], (4, 256))
    att_out[...] = jnp.concatenate([whole[0:4], whole[4:8]], axis=1) + mul * entering

    def drain(i, tw, tn, c):
        first_copy(i, tw, tn, me).wait_send()
        second_copy(i, tw, tn, me).wait_send()
        return c

    others(drain, 0, 1)


def on_device(
    prefit_resid, source_partials, attitude_partials, spline_position, calib_partials, obs_source,
    block_count, obs_range, obs_knot, obs_unit, given_inverse, knot_decay,
):
    wide = lax.axis_size("wide")
    narrow = lax.axis_size("narrow")
    blocks = block_count.shape[0]
    slots = prefit_resid.shape[0]
    count = wide * narrow
    vmem = pl.BlockSpec(memory_space=pltpu.VMEM)
    hbm = pl.BlockSpec(memory_space=pltpu.HBM)
    row = lambda v: v.reshape(1, slots)
    source_update, send = pl.pallas_call(
        functools.partial(local_kernel, blocks, wide, narrow),
        out_shape=(
            jax.ShapeDtypeStruct((5, blocks * SRC_BLK), F32),
            jax.ShapeDtypeStruct((count, 8, 128), F32),
        ),
        in_specs=[pl.BlockSpec(memory_space=pltpu.SMEM)] + [hbm] * 9,
        out_specs=(vmem, vmem),
        scratch_shapes=[
            pltpu.VMEM((8, slots), F32),
            pltpu.VMEM((40 * blocks, 128), F32),
            pltpu.VMEM((8 * blocks, 128), F32),
            pltpu.VMEM((256, 128), BF16),
            pltpu.VMEM((wide * 32, 256), F32),
            pltpu.VMEM((narrow * 2 * 32, 256), F32),
            pltpu.VMEM((1, slots), F32),
            pltpu.VMEM((5, slots), F32),
            pltpu.VMEM((1, slots), jnp.int32),
            pltpu.VMEM((4, slots), F32),
            pltpu.VMEM((1, slots), F32),
            pltpu.VMEM((3, slots), F32),
            pltpu.VMEM((1, slots), jnp.int32),
            pltpu.VMEM((1, slots), jnp.int32),
            pltpu.VMEM((1, slots), jnp.int32),
            pltpu.SemaphoreType.DMA((9,)),
        ],
        compiler_params=pltpu.CompilerParams(vmem_limit_bytes=56 * 1024 * 1024),
        name="local_sums",
    )(
        block_count, row(prefit_resid), source_partials, row(obs_source), attitude_partials,
        row(spline_position), calib_partials, row(obs_range), row(obs_knot), row(obs_unit),
    )
    dma = pltpu.SemaphoreType.DMA
    attitude_update, cal = pl.pallas_call(
        functools.partial(exchange_kernel, wide, narrow),
        out_shape=(
            jax.ShapeDtypeStruct(knot_decay.shape, F32),
            jax.ShapeDtypeStruct((SPLIT, 8, 128), F32),
        ),
        in_specs=[hbm, hbm, hbm],
        out_specs=(vmem, vmem),
        scratch_shapes=[
            pltpu.VMEM((count, 8, 128), F32),
            pltpu.VMEM((2, 8, 128), F32),
            pltpu.VMEM((count, 8, 128), F32),
            pltpu.VMEM((256, 1024), F32),
            pltpu.VMEM(knot_decay.shape, F32),
            dma((count,)), dma((count,)), dma((count,)), dma((count,)), dma((3,)),
        ],
        compiler_params=pltpu.CompilerParams(
            collective_id=0, has_side_effects=True, vmem_limit_bytes=56 * 1024 * 1024
        ),
        name="exchange",
    )(send, given_inverse, knot_decay)
    per = CAL // (narrow * SPLIT)
    cal_update = cal[:, 0:3, 64:64 + per].transpose(1, 0, 2).reshape(3, SPLIT * per)
    return (source_update, attitude_update, cal_update)


def solution(mesh):
    both = P(("wide", "narrow"))
    rows = P(None, ("wide", "narrow"))
    placed = (
        both, rows, rows, both, rows, both, both, both, both, both, P("wide", None, None), P(None, "wide"),
    )
    return jax.shard_map(
        on_device,
        mesh=mesh,
        in_specs=placed,
        out_specs=(rows, P(None, "wide"), P(None, "narrow")),
        check_vma=False,
    )
```

```python
import functools

import jax
import jax.numpy as jnp
from jax import lax
from jax.experimental import pallas as pl
from jax.experimental.pallas import tpu as pltpu
from jax.sharding import PartitionSpec as P

SRC_BLK = 128
SLOT_BLK = 640
CAL = 2016
SPLIT = 8
NT = (((1,), (1,)), ((), ()))
F32 = jnp.float32
BF16 = jnp.bfloat16


def source_row(i, j):
    d = i - j
    return d * 8 + i if d <= 4 else 3 * 8 + j


def ldl_solve(matrix, target):
    n = len(target)
    low = [[None] * n for _ in range(n)]
    inv = [None] * n
    for c in range(n):
        scaled = [low[c][b][1] for b in range(c)]
        d = matrix(c, c) + 1.0
        for b in range(c):
            d = d - scaled[b] * low[c][b][0]
        inv[c] = 1.0 / d
        for r in range(c + 1, n):
            v = matrix(r, c)
            for b in range(c):
                v = v - low[r][b][1] * low[c][b][0]
            low[r][c] = (v * inv[c], v)
    z = []
    for r in range(n):
        v = target[r]
        for b in range(r):
            v = v - low[r][b][0] * z[b]
        z.append(v)
    x = [None] * n
    for r in reversed(range(n)):
        v = z[r] * inv[r]
        for b in range(r + 1, n):
            v = v - low[b][r][0] * x[b]
        x[r] = v
    return x


def split3(v):
    hi = v.astype(BF16).astype(F32)
    rest = v - hi
    mid = rest.astype(BF16).astype(F32)
    return hi, mid, rest - mid


def local_kernel(
    blocks, ranges, narrow,
    count_ref, resid_hbm, sp_hbm, src_hbm, att_hbm, pos_hbm, cal_hbm, rng_hbm, knot_hbm, unit_hbm,
    update_ref, send_ref,
    e_ref, s_ref, x_ref, iota_ref, acc_att, acc_cal,
    resid_ref, sp_ref, src_ref, att_ref, pos_ref, cal_ref, rng_ref, knot_ref, unit_ref, sems,
):
    moves = [
        (resid_hbm, resid_ref), (sp_hbm, sp_ref), (src_hbm, src_ref),
        (att_hbm, att_ref), (pos_hbm, pos_ref), (cal_hbm, cal_ref),
        (rng_hbm, rng_ref), (knot_hbm, knot_ref), (unit_hbm, unit_ref),
    ]
    loads = [pltpu.make_async_copy(a, b, sems.at[k]) for k, (a, b) in enumerate(moves)]
    for load in loads:
        load.start()
    iota_ref[...] = lax.broadcasted_iota(jnp.int32, (256, 128), 0).astype(F32).astype(BF16)
    slot = lax.broadcasted_iota(jnp.int32, (1, SLOT_BLK), 1)
    for load in loads[0:3]:
        load.wait()

    def normals(b, carry):
        at = pl.multiple_of(b * SLOT_BLK, 128)
        cols = pl.ds(at, SLOT_BLK)
        e = jnp.concatenate(
            [sp_ref[:, cols], resid_ref[:, cols], jnp.zeros((2, SLOT_BLK), F32)], axis=0
        )
        live = jnp.broadcast_to(slot < count_ref[b], (8, SLOT_BLK))
        e = jnp.where(live, e, 0.0)
        e_ref[:, cols] = e
        terms = jnp.concatenate(
            [e * e] + [e * pltpu.roll(e, d, axis=0) for d in range(1, 5)], axis=0
        )
        left = jnp.concatenate(split3(terms), axis=0).astype(BF16)
        src = src_ref[:, cols].astype(F32).astype(BF16)
        grid = jnp.concatenate([iota_ref[0:SRC_BLK, :]] * (SLOT_BLK // 128), axis=1)
        hot = jnp.where(grid == src, jnp.ones((), BF16), jnp.zeros((), BF16))
        sums = lax.dot_general(left, hot, NT, preferred_element_type=F32)
        s_ref[pl.ds(b, 40, stride=blocks), :] = sums[0:40] + sums[40:80] + sums[80:120]
        return carry

    lax.fori_loop(0, blocks, normals, 0, unroll=8)

    group = 16
    for g in range(0, blocks, group):
        def entry(i, j, g=g):
            row = source_row(i, j) * blocks + g
            return s_ref[row:row + group, :]

        x = ldl_solve(entry, [entry(5, j) for j in range(5)])
        for p in range(5):
            x_ref[pl.ds(g * 8 + p, group, stride=8), :] = x[p]
        x_ref[pl.ds(g * 8 + 5, group, stride=8), :] = jnp.full((group, 128), -1.0, F32)
        for p in (6, 7):
            x_ref[pl.ds(g * 8 + p, group, stride=8), :] = jnp.zeros((group, 128), F32)

    for load in loads[3:9]:
        load.wait()
    acc_att[...] = jnp.zeros_like(acc_att)
    acc_cal[...] = jnp.zeros_like(acc_cal)
    wide_slots = 2 * SLOT_BLK
    sub8 = lax.broadcasted_iota(jnp.int32, (8, wide_slots), 0)
    first = sub8 < 4
    per = CAL // (narrow * SPLIT)
    per_row = 4 * per

    def horner(u, low, high):
        c = [jnp.where(first, low[i], high[i]) for i in range(4)]
        return c[0] + u * (c[1] + u * (c[2] + u * c[3]))

    def rest(t, carry):
        at = pl.multiple_of(t * wide_slots, 128)
        cols = pl.ds(at, wide_slots)
        src = src_ref[:, cols]
        gathered = []
        for half in range(2):
            b = t * 2 + half
            table = x_ref[pl.ds(pl.multiple_of(b * 8, 8), 8), :]
            update_ref[:, pl.ds(pl.multiple_of(b * 128, 128), 128)] = table[0:5, :]
            for q in range(SLOT_BLK // 128):
                lo = half * SLOT_BLK + q * 128
                ids = jnp.broadcast_to(src[:, lo:lo + 128], (8, 128))
                gathered.append(jnp.take_along_axis(table, ids, axis=1, mode="promise_in_bounds"))
        prod = e_ref[:, cols] * jnp.concatenate(gathered, axis=1)
        prod = prod + pltpu.roll(prod, 4, axis=0)
        prod = prod + pltpu.roll(prod, 2, axis=0)
        prod = prod + pltpu.roll(prod, 1, axis=0)
        after = -prod

        u = jnp.broadcast_to(pos_ref[:, cols], (8, wide_slots))
        sixth = 1.0 / 6.0
        w01 = horner(u, (sixth, -0.5, 0.5, -sixth), (4.0 / 6.0, 0.0, -1.0, 0.5))
        w23 = horner(u, (sixth, 0.5, 0.5, -0.5), (0.0, 0.0, 0.0, sixth))
        att = att_ref[:, cols]
        scaled = jnp.concatenate([att, att], axis=0) * after
        terms = jnp.concatenate([scaled * w01, scaled * w23], axis=0)
        hi = terms.astype(BF16)
        pieces = jnp.concatenate([hi, (terms - hi.astype(F32)).astype(BF16)], axis=0)
        rng = jnp.broadcast_to(rng_ref[:, cols].astype(F32).astype(BF16), (16, wide_slots))
        zero = jnp.zeros((), BF16)
        one = jnp.ones((), BF16)

        def masked(ids, r, parts):
            here = ids == jnp.asarray(r, BF16)
            return [jnp.where(here, parts[k:k + 16], zero) for k in (0, 16)]

        left = jnp.concatenate(
            [v for r in range(ranges) for v in masked(rng, r, pieces)], axis=0
        )
        grid = jnp.concatenate([iota_ref[...]] * (wide_slots // 128), axis=1)
        knot = knot_ref[:, cols].astype(F32).astype(BF16)
        hot = jnp.where(grid == knot, one, zero)
        acc_att[...] += lax.dot_general(left, hot, NT, preferred_element_type=F32)

        slot2 = lax.broadcasted_iota(jnp.int32, (1, SLOT_BLK), 1)
        live = jnp.concatenate(
            [slot2 < count_ref[2 * t], slot2 < count_ref[2 * t + 1]], axis=1
        )
        cal = jnp.where(live, cal_ref[:, cols], 0.0)
        four = jnp.concatenate([cal, after[0:1, :]], axis=0)
        f = jnp.concatenate([four, four], axis=0)
        near = f * jnp.where(first, f, pltpu.roll(f, 1, axis=0))
        far = f * pltpu.roll(f, 2, axis=0)
        far_hi, far_mid, far_lo = split3(far)
        far = jnp.where(sub8 < 2, far_hi, jnp.where(first, far_mid, jnp.where(sub8 < 6, far_lo, 0.0)))
        pieces = jnp.concatenate(list(split3(near)) + [far], axis=0).astype(BF16)
        unit = unit_ref[:, cols]
        upper = (unit * ((1 << 22) // per_row + 1)) >> 22
        place = unit - upper * per_row
        late = [jnp.where(place >= q * per, 64 - per, 0) for q in range(1, 4)]
        place = place + (late[0] + late[1] + late[2])
        upper = jnp.broadcast_to(upper.astype(F32).astype(BF16), (16, wide_slots))
        left = jnp.concatenate(
            [v for r in range(narrow * 2) for v in masked(upper, r, pieces)],
            axis=0,
        )
        hot = jnp.where(grid == place.astype(F32).astype(BF16), one, zero)
        acc_cal[...] += lax.dot_general(left, hot, NT, preferred_element_type=F32)
        return carry

    lax.fori_loop(0, blocks // 2, rest, 0, unroll=4)

    lane = lax.broadcasted_iota(jnp.int32, (4, 256), 1)
    cal_pieces = []
    low = lax.broadcasted_iota(jnp.int32, (5, 128), 1) < 64
    for pair in range(narrow * SPLIT // 2):
        top, half = pair // 2, (pair % 2) * 128
        part = acc_cal[top * 32:(top + 1) * 32, half:half + 128]
        near = part[0:8] + part[8:16] + part[16:24]
        far = part[24:26] + part[26:28] + part[28:30]
        upper5 = near[0:5]
        lower5 = jnp.concatenate([near[5:8], far], axis=0)
        cal_pieces.append(jnp.where(low, upper5, pltpu.roll(lower5, 64, axis=1)))
        cal_pieces.append(jnp.where(low, pltpu.roll(upper5, 64, axis=1), lower5))
    before = None
    for r in range(ranges):
        part = acc_att[r * 32:r * 32 + 16, :] + acc_att[r * 32 + 16:r * 32 + 32, :]
        rolled = [part[0:4]] + [pltpu.roll(part[4 * k:4 * k + 4], k, axis=1) for k in range(1, 4)]
        total = rolled[0]
        for k in range(1, 4):
            wrapped = jnp.zeros((4, 256), F32) if before is None else before[k]
            total = total + jnp.where(lane >= k, rolled[k], wrapped)
        before = rolled
        for n in range(narrow):
            send_ref[n, r, 0:1, :] = total[n:n + 1, 0:128]
            send_ref[n, r, 1:2, :] = total[n:n + 1, 128:256]
            send_ref[n, r, 2:7, :] = cal_pieces[n * SPLIT + r % SPLIT]
            send_ref[n, r, 7:8, :] = jnp.zeros((1, 128), F32)


def exchange_kernel(
    wide, narrow,
    send_ref, inverse_ref, decay_hbm,
    att_out, cal_out,
    recv_a, sum_a, recv_b, near_buf, recv_c, far_buf, recv_d, g_ref, decay_ref,
    send_a, got_a, send_b, got_b, send_c, got_c, send_d, got_d, local_sem,
):
    w = lax.axis_index("wide")
    n = lax.axis_index("narrow")
    mesh_id = pl.DeviceIdType.MESH
    own = pl.ds(pl.multiple_of(n * 256, 256), 256)
    loads = [
        pltpu.make_async_copy(send_ref.at[n], recv_a.at[n], local_sem.at[0]),
        pltpu.make_async_copy(inverse_ref.at[0, own], g_ref, local_sem.at[1]),
        pltpu.make_async_copy(decay_hbm, decay_ref, local_sem.at[2]),
    ]
    for load in loads:
        load.start()

    barrier = pltpu.get_barrier_semaphore()
    narrow_to = [lax.rem(n + i, narrow) for i in range(narrow)]
    wide_to = [lax.rem(w + i, wide) for i in range(wide)]
    for i in range(1, narrow):
        pl.semaphore_signal(barrier, inc=1, device_id=(w, narrow_to[i]), device_id_type=mesh_id)
    for i in range(1, wide):
        pl.semaphore_signal(barrier, inc=1, device_id=(wide_to[i], n), device_id_type=mesh_id)
    pl.semaphore_wait(barrier, narrow + wide - 2)

    def over_narrow(src, dst, send_sem, got_sem, i):
        return pltpu.make_async_remote_copy(
            src_ref=src, dst_ref=dst, send_sem=send_sem.at[i], recv_sem=got_sem,
            device_id=(w, narrow_to[i]), device_id_type=mesh_id,
        )

    def over_wide(src, dst, send_sem, got_sem, i):
        return pltpu.make_async_remote_copy(
            src_ref=src, dst_ref=dst, send_sem=send_sem.at[i], recv_sem=got_sem,
            device_id=(wide_to[i], n), device_id_type=mesh_id,
        )

    sends = [
        over_narrow(send_ref.at[narrow_to[i]], recv_a.at[n], send_a, got_a.at[n], i)
        for i in range(1, narrow)
    ]
    for copy in sends:
        copy.start()
    loads[0].wait()
    for i in range(1, narrow):
        s = narrow_to[i]
        over_narrow(send_ref.at[s], recv_a.at[s], send_a, got_a.at[s], i).wait_recv()
    part = recv_a[0]
    for k in range(1, narrow):
        part = part + recv_a[k]
    sum_a[...] = part

    later = [
        over_wide(sum_a.at[wide_to[i]], recv_b.at[w], send_b, got_b.at[w], i)
        for i in range(1, wide)
    ]
    for copy in later:
        copy.start()
    sends = sends + later
    recv_b[w] = sum_a[w]
    for i in range(1, wide):
        s = wide_to[i]
        over_wide(sum_a.at[s], recv_b.at[s], send_b, got_b.at[s], i).wait_recv()
    total = recv_b[0]
    for k in range(1, wide):
        total = total + recv_b[k]

    for load in loads[1:]:
        load.wait()
    columns = total.T
    y = jnp.zeros((8, 1024), F32)
    for r in range(2):
        prod = columns[:, r:r + 1] * g_ref[r * 128:(r + 1) * 128, :]
        for j in range(16):
            y = y + prod[j * 8:(j + 1) * 8]
    y = jnp.sum(y, axis=0, keepdims=True)
    value = jnp.concatenate([y[:, c * 256:(c + 1) * 256] for c in range(4)], axis=0)
    mul = decay_ref[...]
    add = jnp.sqrt(1.0 - mul * mul) * value
    lane = lax.broadcasted_iota(jnp.int32, (4, 256), 1)
    step = 1
    while step < 256:
        inside = lane >= step
        add = add + mul * jnp.where(inside, pltpu.roll(add, step, axis=1), 0.0)
        mul = mul * jnp.where(inside, pltpu.roll(mul, step, axis=1), 1.0)
        step *= 2
    near_buf[...] = jnp.concatenate([add[:, 0:128], add[:, 128:256]], axis=0)
    later = [
        over_narrow(near_buf, recv_c.at[n], send_c, got_c.at[n], i) for i in range(1, narrow)
    ]
    for copy in later:
        copy.start()
    sends = sends + later
    recv_c[n] = near_buf[...]

    turned = pltpu.roll(total, 64, axis=1)
    q = [total[2 + j:3 + j] for j in range(5)] + [turned[2 + j:3 + j] for j in range(5)]
    pair = {(0, 0): q[0], (1, 1): q[1], (2, 2): q[2], (1, 0): q[5], (2, 1): q[6], (2, 0): q[8]}
    x = ldl_solve(lambda i, j: pair[(i, j)], [q[4], q[9], q[7]])
    x = pltpu.roll(jnp.concatenate(x + [jnp.zeros((5, 128), F32)], axis=0), 64, axis=1)

    for i in range(1, narrow):
        s = narrow_to[i]
        over_narrow(near_buf, recv_c.at[s], send_c, got_c.at[s], i).wait_recv()
    whole = recv_c[0]
    for k in range(1, narrow):
        whole = whole + recv_c[k]
    add = jnp.concatenate([whole[0:4], whole[4:8]], axis=1)
    last = jnp.concatenate(
        [jnp.broadcast_to(add[:, 255:256], (4, 128)), jnp.broadcast_to(mul[:, 255:256], (4, 128))],
        axis=0,
    )
    lane8 = lax.broadcasted_iota(jnp.int32, (8, 128), 1)
    far_buf[...] = jnp.where(lane8 < 64, last, x)
    later = [
        over_wide(far_buf, recv_d.at[w], send_d, got_d.at[w], i) for i in range(1, wide)
    ]
    for copy in later:
        copy.start()
    sends = sends + later
    recv_d[w] = far_buf[...]
    for i in range(1, wide):
        s = wide_to[i]
        over_wide(far_buf, recv_d.at[s], send_d, got_d.at[s], i).wait_recv()

    base = (w // SPLIT) * SPLIT
    for j in range(SPLIT):
        cal_out[j] = recv_d[base + j]
    state = jnp.zeros((4, 128), F32)
    for p in range(wide):
        entry = recv_d[p]
        state = jnp.where(p < w, entry[4:8] * state + entry[0:4], state)
    att_out[...] = add + mul * jnp.broadcast_to(state[:, 0:1], (4, 256))
    for copy in sends:
        copy.wait_send()


def finish_kernel(att_ref, cal_ref, att_out, cal_out):
    att_out[...] = att_ref[...]
    per = cal_out.shape[1] // SPLIT
    cal_out[...] = jnp.concatenate(
        [cal_ref[j, 0:3, 64:64 + per] for j in range(SPLIT)], axis=1
    )


def on_device(
    prefit_resid, source_partials, attitude_partials, spline_position, calib_partials, obs_source,
    block_count, obs_range, obs_knot, obs_unit, given_inverse, knot_decay,
):
    wide = lax.axis_size("wide")
    narrow = lax.axis_size("narrow")
    blocks = block_count.shape[0]
    slots = prefit_resid.shape[0]
    vmem = pl.BlockSpec(memory_space=pltpu.VMEM)
    hbm = pl.BlockSpec(memory_space=pltpu.HBM)
    row = lambda v: v.reshape(1, slots)
    source_update, send = pl.pallas_call(
        functools.partial(local_kernel, blocks, wide, narrow),
        out_shape=(
            jax.ShapeDtypeStruct((5, blocks * SRC_BLK), F32),
            jax.ShapeDtypeStruct((narrow, wide, 8, 128), F32),
        ),
        in_specs=[pl.BlockSpec(memory_space=pltpu.SMEM)] + [hbm] * 9,
        out_specs=(vmem, vmem),
        scratch_shapes=[
            pltpu.VMEM((8, slots), F32),
            pltpu.VMEM((40 * blocks, 128), F32),
            pltpu.VMEM((8 * blocks, 128), F32),
            pltpu.VMEM((256, 128), BF16),
            pltpu.VMEM((wide * 32, 256), F32),
            pltpu.VMEM((narrow * 2 * 32, 256), F32),
            pltpu.VMEM((1, slots), F32),
            pltpu.VMEM((5, slots), F32),
            pltpu.VMEM((1, slots), jnp.int32),
            pltpu.VMEM((4, slots), F32),
            pltpu.VMEM((1, slots), F32),
            pltpu.VMEM((3, slots), F32),
            pltpu.VMEM((1, slots), jnp.int32),
            pltpu.VMEM((1, slots), jnp.int32),
            pltpu.VMEM((1, slots), jnp.int32),
            pltpu.SemaphoreType.DMA((9,)),
        ],
        compiler_params=pltpu.CompilerParams(vmem_limit_bytes=56 * 1024 * 1024),
        name="local_sums",
    )(
        block_count, row(prefit_resid), source_partials, row(obs_source), attitude_partials,
        row(spline_position), calib_partials, row(obs_range), row(obs_knot), row(obs_unit),
    )
    dma = pltpu.SemaphoreType.DMA
    attitude_raw, cal = pl.pallas_call(
        functools.partial(exchange_kernel, wide, narrow),
        out_shape=(
            jax.ShapeDtypeStruct(knot_decay.shape, F32),
            jax.ShapeDtypeStruct((SPLIT, 8, 128), F32),
        ),
        in_specs=[hbm, hbm, hbm],
        out_specs=(vmem, vmem),
        scratch_shapes=[
            pltpu.VMEM((narrow, wide, 8, 128), F32),
            pltpu.VMEM((wide, 8, 128), F32),
            pltpu.VMEM((wide, 8, 128), F32),
            pltpu.VMEM((8, 128), F32),
            pltpu.VMEM((narrow, 8, 128), F32),
            pltpu.VMEM((8, 128), F32),
            pltpu.VMEM((wide, 8, 128), F32),
            pltpu.VMEM((256, 1024), F32),
            pltpu.VMEM(knot_decay.shape, F32),
            dma((narrow,)), dma((narrow,)), dma((wide,)), dma((wide,)),
            dma((narrow,)), dma((narrow,)), dma((wide,)), dma((wide,)),
            dma((3,)),
        ],
        compiler_params=pltpu.CompilerParams(
            collective_id=0, has_side_effects=True, vmem_limit_bytes=56 * 1024 * 1024
        ),
        name="exchange",
    )(send, given_inverse, knot_decay)
    attitude_update, cal_update = pl.pallas_call(
        finish_kernel,
        out_shape=(
            jax.ShapeDtypeStruct(knot_decay.shape, F32),
            jax.ShapeDtypeStruct((3, CAL // narrow), F32),
        ),
        in_specs=[vmem, vmem],
        out_specs=(vmem, vmem),
        compiler_params=pltpu.CompilerParams(vmem_limit_bytes=56 * 1024 * 1024),
        name="finish",
    )(attitude_raw, cal)
    return (source_update, attitude_update, cal_update)


def solution(mesh):
    both = P(("wide", "narrow"))
    rows = P(None, ("wide", "narrow"))
    placed = (
        both, rows, rows, both, rows, both, both, both, both, both, P("wide", None, None), P(None, "wide"),
    )
    return jax.shard_map(
        on_device,
        mesh=mesh,
        in_specs=placed,
        out_specs=(rows, P(None, "wide"), P(None, "narrow")),
        check_vma=False,
    )
```

```python
import functools

import jax
import jax.numpy as jnp
from jax import lax
from jax.experimental import pallas as pl
from jax.experimental.pallas import tpu as pltpu
from jax.sharding import PartitionSpec as P

SRC_BLK = 128
SLOT_BLK = 640
CAL = 2016
SPLIT = 8
NT = (((1,), (1,)), ((), ()))
F32 = jnp.float32
BF16 = jnp.bfloat16


def source_row(i, j):
    d = i - j
    return d * 8 + i if d <= 4 else 3 * 8 + j


def ldl_solve(matrix, target):
    n = len(target)
    low = [[None] * n for _ in range(n)]
    inv = [None] * n
    for c in range(n):
        scaled = [low[c][b][1] for b in range(c)]
        d = matrix(c, c) + 1.0
        for b in range(c):
            d = d - scaled[b] * low[c][b][0]
        inv[c] = 1.0 / d
        for r in range(c + 1, n):
            v = matrix(r, c)
            for b in range(c):
                v = v - low[r][b][1] * low[c][b][0]
            low[r][c] = (v * inv[c], v)
    z = []
    for r in range(n):
        v = target[r]
        for b in range(r):
            v = v - low[r][b][0] * z[b]
        z.append(v)
    x = [None] * n
    for r in reversed(range(n)):
        v = z[r] * inv[r]
        for b in range(r + 1, n):
            v = v - low[b][r][0] * x[b]
        x[r] = v
    return x


def split3(v):
    hi = v.astype(BF16).astype(F32)
    rest = v - hi
    mid = rest.astype(BF16).astype(F32)
    return hi, mid, rest - mid


def source_kernel(
    blocks,
    count_ref, resid_hbm, sp_hbm, src_hbm,
    update_ref, after_ref,
    e_ref, s_ref, x_ref, iota_ref, resid_ref, sp_ref, src_ref, sems,
):
    moves = [(resid_hbm, resid_ref), (sp_hbm, sp_ref), (src_hbm, src_ref)]
    loads = [pltpu.make_async_copy(a, b, sems.at[k]) for k, (a, b) in enumerate(moves)]
    for load in loads:
        load.start()
    iota_ref[...] = lax.broadcasted_iota(jnp.int32, (SRC_BLK, 128), 0).astype(F32).astype(BF16)
    slot = lax.broadcasted_iota(jnp.int32, (1, SLOT_BLK), 1)
    for load in loads:
        load.wait()

    def normals(b, carry):
        at = pl.multiple_of(b * SLOT_BLK, 128)
        cols = pl.ds(at, SLOT_BLK)
        e = jnp.concatenate(
            [sp_ref[:, cols], resid_ref[:, cols], jnp.zeros((2, SLOT_BLK), F32)], axis=0
        )
        live = jnp.broadcast_to(slot < count_ref[b], (8, SLOT_BLK))
        e = jnp.where(live, e, 0.0)
        e_ref[:, cols] = e
        terms = jnp.concatenate(
            [e * e] + [e * pltpu.roll(e, d, axis=0) for d in range(1, 5)], axis=0
        )
        left = jnp.concatenate(split3(terms), axis=0).astype(BF16)
        src = src_ref[:, cols].astype(F32).astype(BF16)
        grid = jnp.concatenate([iota_ref[0:SRC_BLK, :]] * (SLOT_BLK // 128), axis=1)
        hot = jnp.where(grid == src, jnp.ones((), BF16), jnp.zeros((), BF16))
        sums = lax.dot_general(left, hot, NT, preferred_element_type=F32)
        s_ref[pl.ds(b, 40, stride=blocks), :] = sums[0:40] + sums[40:80] + sums[80:120]
        return carry

    lax.fori_loop(0, blocks, normals, 0, unroll=8)

    group = 16
    for g in range(0, blocks, group):
        def entry(i, j, g=g):
            row = source_row(i, j) * blocks + g
            return s_ref[row:row + group, :]

        x = ldl_solve(entry, [entry(5, j) for j in range(5)])
        for p in range(5):
            x_ref[pl.ds(g * 8 + p, group, stride=8), :] = x[p]
        x_ref[pl.ds(g * 8 + 5, group, stride=8), :] = jnp.full((group, 128), -1.0, F32)
        for p in (6, 7):
            x_ref[pl.ds(g * 8 + p, group, stride=8), :] = jnp.zeros((group, 128), F32)

    wide_slots = 2 * SLOT_BLK

    def residuals(t, carry):
        cols = pl.ds(pl.multiple_of(t * wide_slots, 128), wide_slots)
        src = src_ref[:, cols]
        gathered = []
        for half in range(2):
            b = t * 2 + half
            table = x_ref[pl.ds(pl.multiple_of(b * 8, 8), 8), :]
            update_ref[:, pl.ds(pl.multiple_of(b * 128, 128), 128)] = table[0:5, :]
            for q in range(SLOT_BLK // 128):
                lo = half * SLOT_BLK + q * 128
                ids = jnp.broadcast_to(src[:, lo:lo + 128], (8, 128))
                gathered.append(jnp.take_along_axis(table, ids, axis=1, mode="promise_in_bounds"))
        prod = e_ref[:, cols] * jnp.concatenate(gathered, axis=1)
        prod = prod + pltpu.roll(prod, 4, axis=0)
        prod = prod + pltpu.roll(prod, 2, axis=0)
        prod = prod + pltpu.roll(prod, 1, axis=0)
        after_ref[:, cols] = -prod[0:1, :]
        return carry

    lax.fori_loop(0, blocks // 2, residuals, 0, unroll=4)


def knots_kernel(
    blocks, wide, narrow,
    count_ref, after_hbm, att_hbm, pos_hbm, rng_hbm, knot_hbm, cal_hbm, unit_hbm, inverse_ref, decay_hbm,
    att_out, cal_out,
    after_ref, att_ref, pos_ref, rng_ref, knot_ref, cal_ref, unit_ref, g_ref, decay_ref,
    iota_ref, acc_att, acc_cal,
    send_att, recv_a, sum_a, recv_b, near_buf, recv_c, far_buf, recv_d,
    send_cal, recv_e, sum_e, recv_f, unit_buf, recv_g,
    local_sem, send_n, got_n, send_w, got_w,
):
    w = lax.axis_index("wide")
    n = lax.axis_index("narrow")
    mesh_id = pl.DeviceIdType.MESH
    own = pl.ds(pl.multiple_of(n * 256, 256), 256)
    moves = [
        (after_hbm, after_ref), (att_hbm, att_ref), (pos_hbm, pos_ref), (rng_hbm, rng_ref),
        (knot_hbm, knot_ref), (cal_hbm, cal_ref), (unit_hbm, unit_ref),
        (inverse_ref.at[0, own], g_ref), (decay_hbm, decay_ref),
    ]
    loads = [pltpu.make_async_copy(a, b, local_sem.at[k]) for k, (a, b) in enumerate(moves)]
    for load in loads:
        load.start()

    barrier = pltpu.get_barrier_semaphore()
    narrow_to = [lax.rem(n + i, narrow) for i in range(narrow)]
    wide_to = [lax.rem(w + i, wide) for i in range(wide)]
    for i in range(1, narrow):
        pl.semaphore_signal(barrier, inc=1, device_id=(w, narrow_to[i]), device_id_type=mesh_id)
    for i in range(1, wide):
        pl.semaphore_signal(barrier, inc=1, device_id=(wide_to[i], n), device_id_type=mesh_id)

    sent = []

    class Step:
        def __init__(self, along_wide, at, source, slots):
            self.to = wide_to if along_wide else narrow_to
            self.me = w if along_wide else n
            self.out_sem = (send_w if along_wide else send_n).at[at]
            self.in_sem = (got_w if along_wide else got_n).at[at]
            self.along_wide, self.source, self.slots = along_wide, source, slots

        def copy(self, i, slot):
            d = self.to[i]
            return pltpu.make_async_remote_copy(
                src_ref=self.source(d), dst_ref=self.slots.at[slot],
                send_sem=self.out_sem.at[i], recv_sem=self.in_sem.at[slot],
                device_id=(d, n) if self.along_wide else (w, d), device_id_type=mesh_id,
            )

        def start(self):
            for i in range(1, len(self.to)):
                copy = self.copy(i, self.me)
                copy.start()
                sent.append(copy)

        def wait(self):
            for i in range(1, len(self.to)):
                self.copy(i, self.to[i]).wait_recv()

        def total(self):
            self.wait()
            value = self.slots[0]
            for k in range(1, len(self.to)):
                value = value + self.slots[k]
            return value

    iota_ref[...] = lax.broadcasted_iota(jnp.int32, (256, 128), 0).astype(F32).astype(BF16)
    acc_att[...] = jnp.zeros_like(acc_att)
    acc_cal[...] = jnp.zeros_like(acc_cal)
    wide_slots = 2 * SLOT_BLK
    sub8 = lax.broadcasted_iota(jnp.int32, (8, wide_slots), 0)
    first = sub8 < 4
    per = CAL // (narrow * SPLIT)
    per_row = 4 * per
    zero = jnp.zeros((), BF16)
    one = jnp.ones((), BF16)

    def horner(u, low, high):
        c = [jnp.where(first, low[i], high[i]) for i in range(4)]
        return c[0] + u * (c[1] + u * (c[2] + u * c[3]))

    def masked(ids, r, parts):
        here = ids == jnp.asarray(r, BF16)
        return [jnp.where(here, parts[k:k + 16], zero) for k in (0, 16)]

    def summed(acc, ids, count, pieces, place):
        ids = jnp.broadcast_to(ids.astype(F32).astype(BF16), (16, wide_slots))
        left = jnp.concatenate([v for r in range(count) for v in masked(ids, r, pieces)], axis=0)
        grid = jnp.concatenate([iota_ref[...]] * (wide_slots // 128), axis=1)
        hot = jnp.where(grid == place.astype(F32).astype(BF16), one, zero)
        acc[...] += lax.dot_general(left, hot, NT, preferred_element_type=F32)

    def attitude(t, carry):
        cols = pl.ds(pl.multiple_of(t * wide_slots, 128), wide_slots)
        after = jnp.broadcast_to(after_ref[:, cols], (8, wide_slots))
        u = jnp.broadcast_to(pos_ref[:, cols], (8, wide_slots))
        sixth = 1.0 / 6.0
        w01 = horner(u, (sixth, -0.5, 0.5, -sixth), (4.0 / 6.0, 0.0, -1.0, 0.5))
        w23 = horner(u, (sixth, 0.5, 0.5, -0.5), (0.0, 0.0, 0.0, sixth))
        att = att_ref[:, cols]
        scaled = jnp.concatenate([att, att], axis=0) * after
        terms = jnp.concatenate([scaled * w01, scaled * w23], axis=0)
        hi = terms.astype(BF16)
        pieces = jnp.concatenate([hi, (terms - hi.astype(F32)).astype(BF16)], axis=0)
        summed(acc_att, rng_ref[:, cols], wide, pieces, knot_ref[:, cols])
        return carry

    def calibration(t, carry):
        cols = pl.ds(pl.multiple_of(t * wide_slots, 128), wide_slots)
        slot = lax.broadcasted_iota(jnp.int32, (1, SLOT_BLK), 1)
        live = jnp.concatenate([slot < count_ref[2 * t], slot < count_ref[2 * t + 1]], axis=1)
        cal = jnp.where(live, cal_ref[:, cols], 0.0)
        four = jnp.concatenate([cal, after_ref[:, cols]], axis=0)
        f = jnp.concatenate([four, four], axis=0)
        near = f * jnp.where(first, f, pltpu.roll(f, 1, axis=0))
        far = f * pltpu.roll(f, 2, axis=0)
        far_hi, far_mid, far_lo = split3(far)
        far = jnp.where(sub8 < 2, far_hi, jnp.where(first, far_mid, jnp.where(sub8 < 6, far_lo, 0.0)))
        pieces = jnp.concatenate(list(split3(near)) + [far], axis=0).astype(BF16)
        unit = unit_ref[:, cols]
        upper = (unit * ((1 << 22) // per_row + 1)) >> 22
        place = unit - upper * per_row
        late = [jnp.where(place >= q * per, 64 - per, 0) for q in range(1, 4)]
        place = place + (late[0] + late[1] + late[2])
        summed(acc_cal, upper, narrow * 2, pieces, place)
        return carry

    for load in loads[0:5]:
        load.wait()
    turns = blocks // 2
    lax.fori_loop(0, turns, attitude, 0, unroll=4)

    lane = lax.broadcasted_iota(jnp.int32, (4, 256), 1)
    before = None
    for r in range(wide):
        part = acc_att[r * 32:r * 32 + 16, :] + acc_att[r * 32 + 16:r * 32 + 32, :]
        rolled = [part[0:4]] + [pltpu.roll(part[4 * k:4 * k + 4], k, axis=1) for k in range(1, 4)]
        total = rolled[0]
        for k in range(1, 4):
            wrapped = jnp.zeros((4, 256), F32) if before is None else before[k]
            total = total + jnp.where(lane >= k, rolled[k], wrapped)
        before = rolled
        for k in range(narrow):
            send_att[k, r] = jnp.concatenate(
                [total[k:k + 1, 0:128], total[k:k + 1, 128:256], jnp.zeros((6, 128), F32)], axis=0
            )
    pl.semaphore_wait(barrier, narrow + wide - 2)
    step_a = Step(False, 0, lambda d: send_att.at[d], recv_a)
    step_a.start()
    recv_a[n] = send_att[n]
    for load in loads[5:]:
        load.wait()

    quarter = turns // 4
    lax.fori_loop(0, quarter, calibration, 0, unroll=4)

    sum_a[...] = step_a.total()
    step_b = Step(True, 0, lambda d: sum_a.at[d], recv_b)
    step_b.start()
    recv_b[w] = sum_a[w]

    lax.fori_loop(quarter, 2 * quarter, calibration, 0, unroll=4)

    columns = step_b.total().T
    y = jnp.zeros((8, 1024), F32)
    for r in range(2):
        prod = columns[:, r:r + 1] * g_ref[r * 128:(r + 1) * 128, :]
        for j in range(16):
            y = y + prod[j * 8:(j + 1) * 8]
    y = jnp.sum(y, axis=0, keepdims=True)
    value = jnp.concatenate([y[:, c * 256:(c + 1) * 256] for c in range(4)], axis=0)
    mul = decay_ref[...]
    add = jnp.sqrt(1.0 - mul * mul) * value
    step = 1
    while step < 256:
        inside = lane >= step
        add = add + mul * jnp.where(inside, pltpu.roll(add, step, axis=1), 0.0)
        mul = mul * jnp.where(inside, pltpu.roll(mul, step, axis=1), 1.0)
        step *= 2
    near_buf[...] = jnp.concatenate([add[:, 0:128], add[:, 128:256]], axis=0)
    step_c = Step(False, 1, lambda d: near_buf, recv_c)
    step_c.start()
    recv_c[n] = near_buf[...]

    lax.fori_loop(2 * quarter, 3 * quarter, calibration, 0, unroll=4)

    whole = step_c.total()
    add = jnp.concatenate([whole[0:4], whole[4:8]], axis=1)
    far_buf[...] = jnp.concatenate(
        [jnp.broadcast_to(add[:, 255:256], (4, 128)), jnp.broadcast_to(mul[:, 255:256], (4, 128))],
        axis=0,
    )
    step_d = Step(True, 1, lambda d: far_buf, recv_d)
    step_d.start()
    recv_d[w] = far_buf[...]

    lax.fori_loop(3 * quarter, turns, calibration, 0, unroll=4)

    low = lax.broadcasted_iota(jnp.int32, (5, 128), 1) < 64
    pad = jnp.zeros((3, 128), F32)
    units = []
    for pair in range(narrow * SPLIT // 2):
        top, half = pair // 2, (pair % 2) * 128
        part = acc_cal[top * 32:(top + 1) * 32, half:half + 128]
        near = part[0:8] + part[8:16] + part[16:24]
        far = part[24:26] + part[26:28] + part[28:30]
        upper5 = near[0:5]
        lower5 = jnp.concatenate([near[5:8], far], axis=0)
        units.append(jnp.where(low, upper5, pltpu.roll(lower5, 64, axis=1)))
        units.append(jnp.where(low, pltpu.roll(upper5, 64, axis=1), lower5))
    for k in range(narrow):
        for j in range(SPLIT):
            send_cal[k, j] = jnp.concatenate([units[k * SPLIT + j], pad], axis=0)
    step_e = Step(False, 2, lambda d: send_cal.at[d], recv_e)
    step_e.start()
    recv_e[n] = send_cal[n]

    step_d.wait()
    state = jnp.zeros((4, 128), F32)
    for p in range(wide):
        entry = recv_d[p]
        state = jnp.where(p < w, entry[4:8] * state + entry[0:4], state)
    att_out[...] = add + mul * jnp.broadcast_to(state[:, 0:1], (4, 256))

    sum_e[...] = step_e.total()
    step_f = Step(True, 2, lambda d: sum_e.at[lax.rem(d, SPLIT)], recv_f)
    step_f.start()
    recv_f[w] = sum_e[lax.rem(w, SPLIT)]
    total = step_f.total()
    turned = pltpu.roll(total, 64, axis=1)
    q = [total[j:j + 1] for j in range(5)] + [turned[j:j + 1] for j in range(5)]
    pair = {(0, 0): q[0], (1, 1): q[1], (2, 2): q[2], (1, 0): q[5], (2, 1): q[6], (2, 0): q[8]}
    x = ldl_solve(lambda i, j: pair[(i, j)], [q[4], q[9], q[7]])
    unit_buf[...] = jnp.concatenate(x + [jnp.zeros((5, 128), F32)], axis=0)
    step_g = Step(True, 3, lambda d: unit_buf, recv_g)
    step_g.start()
    recv_g[w] = unit_buf[...]
    step_g.wait()
    base = (w // SPLIT) * SPLIT
    for j in range(SPLIT):
        cal_out[j] = recv_g[base + j]
    for copy in sent:
        copy.wait_send()


def finish_kernel(att_ref, cal_ref, att_out, cal_out):
    att_out[...] = att_ref[...]
    per = cal_out.shape[1] // SPLIT
    cal_out[...] = jnp.concatenate(
        [cal_ref[j, 0:3, 0:per] for j in range(SPLIT)], axis=1
    )


def on_device(
    prefit_resid, source_partials, attitude_partials, spline_position, calib_partials, obs_source,
    block_count, obs_range, obs_knot, obs_unit, given_inverse, knot_decay,
):
    wide = lax.axis_size("wide")
    narrow = lax.axis_size("narrow")
    blocks = block_count.shape[0]
    slots = prefit_resid.shape[0]
    vmem = pl.BlockSpec(memory_space=pltpu.VMEM)
    hbm = pl.BlockSpec(memory_space=pltpu.HBM)
    row = lambda v: v.reshape(1, slots)
    limit = 56 * 1024 * 1024
    dma = pltpu.SemaphoreType.DMA
    ints = pltpu.VMEM((1, slots), jnp.int32)
    floats = pltpu.VMEM((1, slots), F32)
    source_update, after = pl.pallas_call(
        functools.partial(source_kernel, blocks),
        out_shape=(
            jax.ShapeDtypeStruct((5, blocks * SRC_BLK), F32),
            jax.ShapeDtypeStruct((1, slots), F32),
        ),
        in_specs=[pl.BlockSpec(memory_space=pltpu.SMEM)] + [hbm] * 3,
        out_specs=(vmem, vmem),
        scratch_shapes=[
            pltpu.VMEM((8, slots), F32),
            pltpu.VMEM((40 * blocks, 128), F32),
            pltpu.VMEM((8 * blocks, 128), F32),
            pltpu.VMEM((SRC_BLK, 128), BF16),
            floats,
            pltpu.VMEM((5, slots), F32),
            ints,
            dma((3,)),
        ],
        compiler_params=pltpu.CompilerParams(vmem_limit_bytes=limit),
        name="sources",
    )(block_count, row(prefit_resid), source_partials, row(obs_source))
    attitude_raw, cal = pl.pallas_call(
        functools.partial(knots_kernel, blocks, wide, narrow),
        out_shape=(
            jax.ShapeDtypeStruct(knot_decay.shape, F32),
            jax.ShapeDtypeStruct((SPLIT, 8, 128), F32),
        ),
        in_specs=[pl.BlockSpec(memory_space=pltpu.SMEM)] + [hbm] * 9,
        out_specs=(vmem, vmem),
        scratch_shapes=[
            floats,
            pltpu.VMEM((4, slots), F32),
            floats, ints, ints,
            pltpu.VMEM((3, slots), F32),
            ints,
            pltpu.VMEM((256, 1024), F32),
            pltpu.VMEM(knot_decay.shape, F32),
            pltpu.VMEM((256, 128), BF16),
            pltpu.VMEM((wide * 32, 256), F32),
            pltpu.VMEM((narrow * 2 * 32, 256), F32),
            pltpu.VMEM((narrow, wide, 8, 128), F32),
            pltpu.VMEM((narrow, wide, 8, 128), F32),
            pltpu.VMEM((wide, 8, 128), F32),
            pltpu.VMEM((wide, 8, 128), F32),
            pltpu.VMEM((8, 128), F32),
            pltpu.VMEM((narrow, 8, 128), F32),
            pltpu.VMEM((8, 128), F32),
            pltpu.VMEM((wide, 8, 128), F32),
            pltpu.VMEM((narrow, SPLIT, 8, 128), F32),
            pltpu.VMEM((narrow, SPLIT, 8, 128), F32),
            pltpu.VMEM((SPLIT, 8, 128), F32),
            pltpu.VMEM((wide, 8, 128), F32),
            pltpu.VMEM((8, 128), F32),
            pltpu.VMEM((wide, 8, 128), F32),
            dma((9,)),
            dma((3, narrow)), dma((3, narrow)), dma((4, wide)), dma((4, wide)),
        ],
        compiler_params=pltpu.CompilerParams(
            collective_id=0, has_side_effects=True, vmem_limit_bytes=limit
        ),
        name="knots_units",
    )(
        block_count, after, attitude_partials, row(spline_position), row(obs_range), row(obs_knot),
        calib_partials, row(obs_unit), given_inverse, knot_decay,
    )
    attitude_update, cal_update = pl.pallas_call(
        finish_kernel,
        out_shape=(
            jax.ShapeDtypeStruct(knot_decay.shape, F32),
            jax.ShapeDtypeStruct((3, CAL // narrow), F32),
        ),
        in_specs=[vmem, vmem],
        out_specs=(vmem, vmem),
        compiler_params=pltpu.CompilerParams(vmem_limit_bytes=56 * 1024 * 1024),
        name="finish",
    )(attitude_raw, cal)
    return (source_update, attitude_update, cal_update)


def solution(mesh):
    both = P(("wide", "narrow"))
    rows = P(None, ("wide", "narrow"))
    placed = (
        both, rows, rows, both, rows, both, both, both, both, both, P("wide", None, None), P(None, "wide"),
    )
    return jax.shard_map(
        on_device,
        mesh=mesh,
        in_specs=placed,
        out_specs=(rows, P(None, "wide"), P(None, "narrow")),
        check_vma=False,
    )
```

```python
import functools

import jax
import jax.numpy as jnp
from jax import lax
from jax.experimental import pallas as pl
from jax.experimental.pallas import tpu as pltpu
from jax.sharding import PartitionSpec as P

SRC_BLK = 128
SLOT_BLK = 640
CAL = 2016
SPLIT = 8
NT = (((1,), (1,)), ((), ()))
F32 = jnp.float32
BF16 = jnp.bfloat16


def source_row(i, j):
    d = i - j
    return d * 8 + i if d <= 4 else 3 * 8 + j


def ldl_solve(matrix, target):
    n = len(target)
    low = [[None] * n for _ in range(n)]
    inv = [None] * n
    for c in range(n):
        scaled = [low[c][b][1] for b in range(c)]
        d = matrix(c, c) + 1.0
        for b in range(c):
            d = d - scaled[b] * low[c][b][0]
        inv[c] = 1.0 / d
        for r in range(c + 1, n):
            v = matrix(r, c)
            for b in range(c):
                v = v - low[r][b][1] * low[c][b][0]
            low[r][c] = (v * inv[c], v)
    z = []
    for r in range(n):
        v = target[r]
        for b in range(r):
            v = v - low[r][b][0] * z[b]
        z.append(v)
    x = [None] * n
    for r in reversed(range(n)):
        v = z[r] * inv[r]
        for b in range(r + 1, n):
            v = v - low[b][r][0] * x[b]
        x[r] = v
    return x


def split3(v):
    hi = v.astype(BF16).astype(F32)
    rest = v - hi
    mid = rest.astype(BF16).astype(F32)
    return hi, mid, rest - mid


def source_kernel(
    blocks,
    count_ref, resid_hbm, sp_hbm, src_hbm,
    update_ref, after_ref,
    e_ref, s_ref, x_ref, iota_ref, resid_ref, sp_ref, src_ref, sems,
):
    moves = [(resid_hbm, resid_ref), (sp_hbm, sp_ref), (src_hbm, src_ref)]
    loads = [pltpu.make_async_copy(a, b, sems.at[k]) for k, (a, b) in enumerate(moves)]
    for load in loads:
        load.start()
    iota_ref[...] = lax.broadcasted_iota(jnp.int32, (SRC_BLK, 128), 0).astype(F32).astype(BF16)
    slot = lax.broadcasted_iota(jnp.int32, (1, SLOT_BLK), 1)
    for load in loads:
        load.wait()

    def normals(b, carry):
        at = pl.multiple_of(b * SLOT_BLK, 128)
        cols = pl.ds(at, SLOT_BLK)
        e = jnp.concatenate(
            [sp_ref[:, cols], resid_ref[:, cols], jnp.zeros((2, SLOT_BLK), F32)], axis=0
        )
        live = jnp.broadcast_to(slot < count_ref[b], (8, SLOT_BLK))
        e = jnp.where(live, e, 0.0)
        e_ref[:, cols] = e
        terms = jnp.concatenate(
            [e * e] + [e * pltpu.roll(e, d, axis=0) for d in range(1, 5)], axis=0
        )
        left = jnp.concatenate(split3(terms), axis=0).astype(BF16)
        src = src_ref[:, cols].astype(F32).astype(BF16)
        grid = jnp.concatenate([iota_ref[0:SRC_BLK, :]] * (SLOT_BLK // 128), axis=1)
        hot = jnp.where(grid == src, jnp.ones((), BF16), jnp.zeros((), BF16))
        sums = lax.dot_general(left, hot, NT, preferred_element_type=F32)
        s_ref[pl.ds(b, 40, stride=blocks), :] = sums[0:40] + sums[40:80] + sums[80:120]
        return carry

    lax.fori_loop(0, blocks, normals, 0, unroll=8)

    group = 16
    for g in range(0, blocks, group):
        def entry(i, j, g=g):
            row = source_row(i, j) * blocks + g
            return s_ref[row:row + group, :]

        x = ldl_solve(entry, [entry(5, j) for j in range(5)])
        for p in range(5):
            x_ref[pl.ds(g * 8 + p, group, stride=8), :] = x[p]
        x_ref[pl.ds(g * 8 + 5, group, stride=8), :] = jnp.full((group, 128), -1.0, F32)
        for p in (6, 7):
            x_ref[pl.ds(g * 8 + p, group, stride=8), :] = jnp.zeros((group, 128), F32)

    wide_slots = 2 * SLOT_BLK

    def residuals(t, carry):
        cols = pl.ds(pl.multiple_of(t * wide_slots, 128), wide_slots)
        src = src_ref[:, cols]
        gathered = []
        for half in range(2):
            b = t * 2 + half
            table = x_ref[pl.ds(pl.multiple_of(b * 8, 8), 8), :]
            update_ref[:, pl.ds(pl.multiple_of(b * 128, 128), 128)] = table[0:5, :]
            for q in range(SLOT_BLK // 128):
                lo = half * SLOT_BLK + q * 128
                ids = jnp.broadcast_to(src[:, lo:lo + 128], (8, 128))
                gathered.append(jnp.take_along_axis(table, ids, axis=1, mode="promise_in_bounds"))
        prod = e_ref[:, cols] * jnp.concatenate(gathered, axis=1)
        prod = prod + pltpu.roll(prod, 4, axis=0)
        prod = prod + pltpu.roll(prod, 2, axis=0)
        prod = prod + pltpu.roll(prod, 1, axis=0)
        after_ref[:, cols] = -prod[0:1, :]
        return carry

    lax.fori_loop(0, blocks // 2, residuals, 0, unroll=4)


def knots_kernel(
    blocks, wide, narrow,
    count_ref, after_hbm, att_hbm, pos_hbm, rng_hbm, knot_hbm, cal_hbm, unit_hbm, inverse_ref, decay_hbm,
    att_out, cal_out,
    after_ref, att_ref, pos_ref, rng_ref, knot_ref, cal_ref, unit_ref, g_ref, decay_ref, mul_ref, add_ref,
    iota_ref, acc_att, acc_cal,
    send_att, recv_a, sum_a, recv_b, near_buf, recv_c, far_buf, recv_d,
    send_cal, recv_e, sum_e, recv_f, unit_buf, recv_g,
    local_sem, send_n, got_n, send_w, got_w,
):
    w = lax.axis_index("wide")
    n = lax.axis_index("narrow")
    mesh_id = pl.DeviceIdType.MESH
    own = pl.ds(pl.multiple_of(n * 256, 256), 256)
    moves = [
        (after_hbm, after_ref), (att_hbm, att_ref), (pos_hbm, pos_ref), (rng_hbm, rng_ref),
        (knot_hbm, knot_ref), (cal_hbm, cal_ref), (unit_hbm, unit_ref),
        (inverse_ref.at[0, own], g_ref), (decay_hbm, decay_ref),
    ]
    loads = [pltpu.make_async_copy(a, b, local_sem.at[k]) for k, (a, b) in enumerate(moves)]
    for load in loads:
        load.start()

    barrier = pltpu.get_barrier_semaphore()
    narrow_to = [lax.rem(n + i, narrow) for i in range(narrow)]
    wide_to = [lax.rem(w + i, wide) for i in range(wide)]
    for i in range(1, narrow):
        pl.semaphore_signal(barrier, inc=1, device_id=(w, narrow_to[i]), device_id_type=mesh_id)
    for i in range(1, wide):
        pl.semaphore_signal(barrier, inc=1, device_id=(wide_to[i], n), device_id_type=mesh_id)

    sent = []

    class Step:
        def __init__(self, along_wide, at, source, slots):
            self.to = wide_to if along_wide else narrow_to
            self.me = w if along_wide else n
            self.out_sem = (send_w if along_wide else send_n).at[at]
            self.in_sem = (got_w if along_wide else got_n).at[at]
            self.along_wide, self.source, self.slots = along_wide, source, slots
            self.copies = [self.copy(i, self.me) for i in range(1, len(self.to))]
            self.arrivals = [self.copy(i, self.to[i]) for i in range(1, len(self.to))]
            sent.extend(self.copies)

        def copy(self, i, slot):
            d = self.to[i]
            return pltpu.make_async_remote_copy(
                src_ref=self.source(d), dst_ref=self.slots.at[slot],
                send_sem=self.out_sem.at[i], recv_sem=self.in_sem.at[slot],
                device_id=(d, n) if self.along_wide else (w, d), device_id_type=mesh_id,
            )

        def start(self):
            for copy in self.copies:
                copy.start()

        def wait(self):
            for copy in self.arrivals:
                copy.wait_recv()

        def total(self):
            self.wait()
            value = self.slots[0]
            for k in range(1, len(self.to)):
                value = value + self.slots[k]
            return value

    iota_ref[...] = lax.broadcasted_iota(jnp.int32, (256, 128), 0).astype(F32).astype(BF16)
    acc_att[...] = jnp.zeros_like(acc_att)
    acc_cal[...] = jnp.zeros_like(acc_cal)
    wide_slots = 2 * SLOT_BLK
    sub8 = lax.broadcasted_iota(jnp.int32, (8, wide_slots), 0)
    first = sub8 < 4
    per = CAL // (narrow * SPLIT)
    per_row = 4 * per
    zero = jnp.zeros((), BF16)
    one = jnp.ones((), BF16)

    def horner(u, low, high):
        c = [jnp.where(first, low[i], high[i]) for i in range(4)]
        return c[0] + u * (c[1] + u * (c[2] + u * c[3]))

    def masked(ids, r, parts):
        here = ids == jnp.asarray(r, BF16)
        return [jnp.where(here, parts[k:k + 16], zero) for k in (0, 16)]

    def summed(acc, ids, count, pieces, place):
        ids = jnp.broadcast_to(ids.astype(F32).astype(BF16), (16, wide_slots))
        left = jnp.concatenate([v for r in range(count) for v in masked(ids, r, pieces)], axis=0)
        grid = jnp.concatenate([iota_ref[...]] * (wide_slots // 128), axis=1)
        hot = jnp.where(grid == place.astype(F32).astype(BF16), one, zero)
        acc[...] += lax.dot_general(left, hot, NT, preferred_element_type=F32)

    def attitude(t, carry):
        cols = pl.ds(pl.multiple_of(t * wide_slots, 128), wide_slots)
        after = jnp.broadcast_to(after_ref[:, cols], (8, wide_slots))
        u = jnp.broadcast_to(pos_ref[:, cols], (8, wide_slots))
        sixth = 1.0 / 6.0
        w01 = horner(u, (sixth, -0.5, 0.5, -sixth), (4.0 / 6.0, 0.0, -1.0, 0.5))
        w23 = horner(u, (sixth, 0.5, 0.5, -0.5), (0.0, 0.0, 0.0, sixth))
        att = att_ref[:, cols]
        scaled = jnp.concatenate([att, att], axis=0) * after
        terms = jnp.concatenate([scaled * w01, scaled * w23], axis=0)
        hi = terms.astype(BF16)
        pieces = jnp.concatenate([hi, (terms - hi.astype(F32)).astype(BF16)], axis=0)
        summed(acc_att, rng_ref[:, cols], wide, pieces, knot_ref[:, cols])
        return carry

    def calibration(t, carry):
        cols = pl.ds(pl.multiple_of(t * wide_slots, 128), wide_slots)
        slot = lax.broadcasted_iota(jnp.int32, (1, SLOT_BLK), 1)
        live = jnp.concatenate([slot < count_ref[2 * t], slot < count_ref[2 * t + 1]], axis=1)
        cal = jnp.where(live, cal_ref[:, cols], 0.0)
        four = jnp.concatenate([cal, after_ref[:, cols]], axis=0)
        f = jnp.concatenate([four, four], axis=0)
        near = f * jnp.where(first, f, pltpu.roll(f, 1, axis=0))
        far = f * pltpu.roll(f, 2, axis=0)
        far_hi, far_mid, far_lo = split3(far)
        far = jnp.where(sub8 < 2, far_hi, jnp.where(first, far_mid, jnp.where(sub8 < 6, far_lo, 0.0)))
        pieces = jnp.concatenate(list(split3(near)) + [far], axis=0).astype(BF16)
        unit = unit_ref[:, cols]
        upper = (unit * ((1 << 22) // per_row + 1)) >> 22
        place = unit - upper * per_row
        late = [jnp.where(place >= q * per, 64 - per, 0) for q in range(1, 4)]
        place = place + (late[0] + late[1] + late[2])
        summed(acc_cal, upper, narrow * 2, pieces, place)
        return carry

    for load in loads[0:5]:
        load.wait()
    turns = blocks // 2
    lax.fori_loop(0, turns, attitude, 0, unroll=4)

    lane = lax.broadcasted_iota(jnp.int32, (4, 256), 1)
    before = None
    for r in range(wide):
        part = acc_att[r * 32:r * 32 + 16, :] + acc_att[r * 32 + 16:r * 32 + 32, :]
        rolled = [part[0:4]] + [pltpu.roll(part[4 * k:4 * k + 4], k, axis=1) for k in range(1, 4)]
        total = rolled[0]
        for k in range(1, 4):
            wrapped = jnp.zeros((4, 256), F32) if before is None else before[k]
            total = total + jnp.where(lane >= k, rolled[k], wrapped)
        before = rolled
        for k in range(narrow):
            send_att[k, r] = jnp.concatenate(
                [total[k:k + 1, 0:128], total[k:k + 1, 128:256], jnp.zeros((6, 128), F32)], axis=0
            )
    pl.semaphore_wait(barrier, narrow + wide - 2)
    step_a = Step(False, 0, lambda d: send_att.at[d], recv_a)
    step_a.start()
    recv_a[n] = send_att[n]
    for load in loads[5:]:
        load.wait()

    step_b = Step(True, 0, lambda d: sum_a.at[d], recv_b)
    step_c = Step(False, 1, lambda d: near_buf, recv_c)
    step_d = Step(True, 1, lambda d: far_buf, recv_d)

    def after_first():
        sum_a[...] = step_a.total()
        step_b.start()
        recv_b[w] = sum_a[w]

    def after_second():
        columns = step_b.total().T
        y = jnp.zeros((8, 1024), F32)
        for r in range(2):
            prod = columns[:, r:r + 1] * g_ref[r * 128:(r + 1) * 128, :]
            for j in range(16):
                y = y + prod[j * 8:(j + 1) * 8]
        y = jnp.sum(y, axis=0, keepdims=True)
        value = jnp.concatenate([y[:, c * 256:(c + 1) * 256] for c in range(4)], axis=0)
        mul = decay_ref[...]
        add = jnp.sqrt(1.0 - mul * mul) * value
        step = 1
        while step < 256:
            inside = lane >= step
            add = add + mul * jnp.where(inside, pltpu.roll(add, step, axis=1), 0.0)
            mul = mul * jnp.where(inside, pltpu.roll(mul, step, axis=1), 1.0)
            step *= 2
        mul_ref[...] = mul
        near_buf[...] = jnp.concatenate([add[:, 0:128], add[:, 128:256]], axis=0)
        step_c.start()
        recv_c[n] = near_buf[...]

    def after_third():
        whole = step_c.total()
        add = jnp.concatenate([whole[0:4], whole[4:8]], axis=1)
        add_ref[...] = add
        mul = mul_ref[...]
        far_buf[...] = jnp.concatenate(
            [jnp.broadcast_to(add[:, 255:256], (4, 128)), jnp.broadcast_to(mul[:, 255:256], (4, 128))],
            axis=0,
        )
        step_d.start()
        recv_d[w] = far_buf[...]

    quarter = turns // 4

    def quarters(at, carry):
        def one_turn(t, c):
            return calibration(at * quarter + t, c)

        lax.fori_loop(0, quarter, one_turn, 0, unroll=4)
        pl.when(at == 0)(after_first)
        pl.when(at == 1)(after_second)
        pl.when(at == 2)(after_third)
        return carry

    lax.fori_loop(0, 4, quarters, 0)

    low = lax.broadcasted_iota(jnp.int32, (5, 128), 1) < 64
    pad = jnp.zeros((3, 128), F32)
    units = []
    for pair in range(narrow * SPLIT // 2):
        top, half = pair // 2, (pair % 2) * 128
        part = acc_cal[top * 32:(top + 1) * 32, half:half + 128]
        near = part[0:8] + part[8:16] + part[16:24]
        far = part[24:26] + part[26:28] + part[28:30]
        upper5 = near[0:5]
        lower5 = jnp.concatenate([near[5:8], far], axis=0)
        units.append(jnp.where(low, upper5, pltpu.roll(lower5, 64, axis=1)))
        units.append(jnp.where(low, pltpu.roll(upper5, 64, axis=1), lower5))
    for k in range(narrow):
        for j in range(SPLIT):
            send_cal[k, j] = jnp.concatenate([units[k * SPLIT + j], pad], axis=0)
    step_e = Step(False, 2, lambda d: send_cal.at[d], recv_e)
    step_e.start()
    recv_e[n] = send_cal[n]

    step_d.wait()
    state = jnp.zeros((4, 128), F32)
    for p in range(wide):
        entry = recv_d[p]
        state = jnp.where(p < w, entry[4:8] * state + entry[0:4], state)
    att_out[...] = add_ref[...] + mul_ref[...] * jnp.broadcast_to(state[:, 0:1], (4, 256))

    sum_e[...] = step_e.total()
    step_f = Step(True, 2, lambda d: sum_e.at[lax.rem(d, SPLIT)], recv_f)
    step_f.start()
    recv_f[w] = sum_e[lax.rem(w, SPLIT)]
    total = step_f.total()
    turned = pltpu.roll(total, 64, axis=1)
    q = [total[j:j + 1] for j in range(5)] + [turned[j:j + 1] for j in range(5)]
    pair = {(0, 0): q[0], (1, 1): q[1], (2, 2): q[2], (1, 0): q[5], (2, 1): q[6], (2, 0): q[8]}
    x = ldl_solve(lambda i, j: pair[(i, j)], [q[4], q[9], q[7]])
    unit_buf[...] = jnp.concatenate(x + [jnp.zeros((5, 128), F32)], axis=0)
    step_g = Step(True, 3, lambda d: unit_buf, recv_g)
    step_g.start()
    recv_g[w] = unit_buf[...]
    step_g.wait()
    base = (w // SPLIT) * SPLIT
    for j in range(SPLIT):
        cal_out[j] = recv_g[base + j]
    for copy in sent:
        copy.wait_send()


def finish_kernel(att_ref, cal_ref, att_out, cal_out):
    att_out[...] = att_ref[...]
    per = cal_out.shape[1] // SPLIT
    cal_out[...] = jnp.concatenate(
        [cal_ref[j, 0:3, 0:per] for j in range(SPLIT)], axis=1
    )


def on_device(
    prefit_resid, source_partials, attitude_partials, spline_position, calib_partials, obs_source,
    block_count, obs_range, obs_knot, obs_unit, given_inverse, knot_decay,
):
    wide = lax.axis_size("wide")
    narrow = lax.axis_size("narrow")
    blocks = block_count.shape[0]
    slots = prefit_resid.shape[0]
    vmem = pl.BlockSpec(memory_space=pltpu.VMEM)
    hbm = pl.BlockSpec(memory_space=pltpu.HBM)
    row = lambda v: v.reshape(1, slots)
    limit = 56 * 1024 * 1024
    dma = pltpu.SemaphoreType.DMA
    ints = pltpu.VMEM((1, slots), jnp.int32)
    floats = pltpu.VMEM((1, slots), F32)
    source_update, after = pl.pallas_call(
        functools.partial(source_kernel, blocks),
        out_shape=(
            jax.ShapeDtypeStruct((5, blocks * SRC_BLK), F32),
            jax.ShapeDtypeStruct((1, slots), F32),
        ),
        in_specs=[pl.BlockSpec(memory_space=pltpu.SMEM)] + [hbm] * 3,
        out_specs=(vmem, vmem),
        scratch_shapes=[
            pltpu.VMEM((8, slots), F32),
            pltpu.VMEM((40 * blocks, 128), F32),
            pltpu.VMEM((8 * blocks, 128), F32),
            pltpu.VMEM((SRC_BLK, 128), BF16),
            floats,
            pltpu.VMEM((5, slots), F32),
            ints,
            dma((3,)),
        ],
        compiler_params=pltpu.CompilerParams(vmem_limit_bytes=limit),
        name="sources",
    )(block_count, row(prefit_resid), source_partials, row(obs_source))
    attitude_raw, cal = pl.pallas_call(
        functools.partial(knots_kernel, blocks, wide, narrow),
        out_shape=(
            jax.ShapeDtypeStruct(knot_decay.shape, F32),
            jax.ShapeDtypeStruct((SPLIT, 8, 128), F32),
        ),
        in_specs=[pl.BlockSpec(memory_space=pltpu.SMEM)] + [hbm] * 9,
        out_specs=(vmem, vmem),
        scratch_shapes=[
            floats,
            pltpu.VMEM((4, slots), F32),
            floats, ints, ints,
            pltpu.VMEM((3, slots), F32),
            ints,
            pltpu.VMEM((256, 1024), F32),
            pltpu.VMEM(knot_decay.shape, F32),
            pltpu.VMEM(knot_decay.shape, F32),
            pltpu.VMEM(knot_decay.shape, F32),
            pltpu.VMEM((256, 128), BF16),
            pltpu.VMEM((wide * 32, 256), F32),
            pltpu.VMEM((narrow * 2 * 32, 256), F32),
            pltpu.VMEM((narrow, wide, 8, 128), F32),
            pltpu.VMEM((narrow, wide, 8, 128), F32),
            pltpu.VMEM((wide, 8, 128), F32),
            pltpu.VMEM((wide, 8, 128), F32),
            pltpu.VMEM((8, 128), F32),
            pltpu.VMEM((narrow, 8, 128), F32),
            pltpu.VMEM((8, 128), F32),
            pltpu.VMEM((wide, 8, 128), F32),
            pltpu.VMEM((narrow, SPLIT, 8, 128), F32),
            pltpu.VMEM((narrow, SPLIT, 8, 128), F32),
            pltpu.VMEM((SPLIT, 8, 128), F32),
            pltpu.VMEM((wide, 8, 128), F32),
            pltpu.VMEM((8, 128), F32),
            pltpu.VMEM((wide, 8, 128), F32),
            dma((9,)),
            dma((3, narrow)), dma((3, narrow)), dma((4, wide)), dma((4, wide)),
        ],
        compiler_params=pltpu.CompilerParams(
            collective_id=0, has_side_effects=True, vmem_limit_bytes=limit
        ),
        name="knots_units",
    )(
        block_count, after, attitude_partials, row(spline_position), row(obs_range), row(obs_knot),
        calib_partials, row(obs_unit), given_inverse, knot_decay,
    )
    attitude_update, cal_update = pl.pallas_call(
        finish_kernel,
        out_shape=(
            jax.ShapeDtypeStruct(knot_decay.shape, F32),
            jax.ShapeDtypeStruct((3, CAL // narrow), F32),
        ),
        in_specs=[vmem, vmem],
        out_specs=(vmem, vmem),
        compiler_params=pltpu.CompilerParams(vmem_limit_bytes=56 * 1024 * 1024),
        name="finish",
    )(attitude_raw, cal)
    return (source_update, attitude_update, cal_update)


def solution(mesh):
    both = P(("wide", "narrow"))
    rows = P(None, ("wide", "narrow"))
    placed = (
        both, rows, rows, both, rows, both, both, both, both, both, P("wide", None, None), P(None, "wide"),
    )
    return jax.shard_map(
        on_device,
        mesh=mesh,
        in_specs=placed,
        out_specs=(rows, P(None, "wide"), P(None, "narrow")),
        check_vma=False,
    )
```

```python
import functools

import jax
import jax.numpy as jnp
from jax import lax
from jax.experimental import pallas as pl
from jax.experimental.pallas import tpu as pltpu
from jax.sharding import PartitionSpec as P

SRC_BLK = 128
SLOT_BLK = 640
CAL = 2016
SPLIT = 8
NT = (((1,), (1,)), ((), ()))
F32 = jnp.float32
BF16 = jnp.bfloat16


def source_row(i, j):
    d = i - j
    return d * 8 + i if d <= 4 else 3 * 8 + j


def ldl_solve(matrix, target):
    n = len(target)
    low = [[None] * n for _ in range(n)]
    inv = [None] * n
    for c in range(n):
        scaled = [low[c][b][1] for b in range(c)]
        d = matrix(c, c) + 1.0
        for b in range(c):
            d = d - scaled[b] * low[c][b][0]
        inv[c] = 1.0 / d
        for r in range(c + 1, n):
            v = matrix(r, c)
            for b in range(c):
                v = v - low[r][b][1] * low[c][b][0]
            low[r][c] = (v * inv[c], v)
    z = []
    for r in range(n):
        v = target[r]
        for b in range(r):
            v = v - low[r][b][0] * z[b]
        z.append(v)
    x = [None] * n
    for r in reversed(range(n)):
        v = z[r] * inv[r]
        for b in range(r + 1, n):
            v = v - low[b][r][0] * x[b]
        x[r] = v
    return x


def split3(v):
    hi = v.astype(BF16).astype(F32)
    rest = v - hi
    mid = rest.astype(BF16).astype(F32)
    return hi, mid, rest - mid


def source_kernel(
    blocks,
    count_ref, resid_hbm, sp_hbm, src_hbm,
    update_ref, after_ref,
    e_ref, s_ref, x_ref, iota_ref, resid_ref, sp_ref, src_ref, sems,
):
    moves = [(resid_hbm, resid_ref), (sp_hbm, sp_ref), (src_hbm, src_ref)]
    loads = [pltpu.make_async_copy(a, b, sems.at[k]) for k, (a, b) in enumerate(moves)]
    for load in loads:
        load.start()
    iota_ref[...] = lax.broadcasted_iota(jnp.int32, (SRC_BLK, 128), 0).astype(F32).astype(BF16)
    slot = lax.broadcasted_iota(jnp.int32, (1, SLOT_BLK), 1)
    for load in loads:
        load.wait()

    def normals(b, carry):
        at = pl.multiple_of(b * SLOT_BLK, 128)
        cols = pl.ds(at, SLOT_BLK)
        e = jnp.concatenate(
            [sp_ref[:, cols], resid_ref[:, cols], jnp.zeros((2, SLOT_BLK), F32)], axis=0
        )
        live = jnp.broadcast_to(slot < count_ref[b], (8, SLOT_BLK))
        e = jnp.where(live, e, 0.0)
        e_ref[:, cols] = e
        terms = jnp.concatenate(
            [e * e] + [e * pltpu.roll(e, d, axis=0) for d in range(1, 5)], axis=0
        )
        left = jnp.concatenate(split3(terms), axis=0).astype(BF16)
        src = src_ref[:, cols].astype(F32).astype(BF16)
        grid = jnp.concatenate([iota_ref[0:SRC_BLK, :]] * (SLOT_BLK // 128), axis=1)
        hot = jnp.where(grid == src, jnp.ones((), BF16), jnp.zeros((), BF16))
        sums = lax.dot_general(left, hot, NT, preferred_element_type=F32)
        s_ref[pl.ds(b, 40, stride=blocks), :] = sums[0:40] + sums[40:80] + sums[80:120]
        return carry

    lax.fori_loop(0, blocks, normals, 0, unroll=8)

    group = 16
    for g in range(0, blocks, group):
        def entry(i, j, g=g):
            row = source_row(i, j) * blocks + g
            return s_ref[row:row + group, :]

        x = ldl_solve(entry, [entry(5, j) for j in range(5)])
        for p in range(5):
            x_ref[pl.ds(g * 8 + p, group, stride=8), :] = x[p]
        x_ref[pl.ds(g * 8 + 5, group, stride=8), :] = jnp.full((group, 128), -1.0, F32)
        for p in (6, 7):
            x_ref[pl.ds(g * 8 + p, group, stride=8), :] = jnp.zeros((group, 128), F32)

    wide_slots = 2 * SLOT_BLK

    def residuals(t, carry):
        cols = pl.ds(pl.multiple_of(t * wide_slots, 128), wide_slots)
        src = src_ref[:, cols]
        gathered = []
        for half in range(2):
            b = t * 2 + half
            table = x_ref[pl.ds(pl.multiple_of(b * 8, 8), 8), :]
            update_ref[:, pl.ds(pl.multiple_of(b * 128, 128), 128)] = table[0:5, :]
            for q in range(SLOT_BLK // 128):
                lo = half * SLOT_BLK + q * 128
                ids = jnp.broadcast_to(src[:, lo:lo + 128], (8, 128))
                gathered.append(jnp.take_along_axis(table, ids, axis=1, mode="promise_in_bounds"))
        prod = e_ref[:, cols] * jnp.concatenate(gathered, axis=1)
        prod = prod + pltpu.roll(prod, 4, axis=0)
        prod = prod + pltpu.roll(prod, 2, axis=0)
        prod = prod + pltpu.roll(prod, 1, axis=0)
        after_ref[:, cols] = -prod[0:1, :]
        return carry

    lax.fori_loop(0, blocks // 2, residuals, 0, unroll=4)


def knots_kernel(
    blocks, wide, narrow,
    count_ref, after_hbm, att_hbm, pos_hbm, rng_hbm, knot_hbm, cal_hbm, unit_hbm, inverse_ref, decay_hbm,
    att_out, cal_out,
    after_ref, att_ref, pos_ref, rng_ref, knot_ref, cal_ref, unit_ref, g_ref, decay_ref,
    iota_ref, acc_att, acc_cal,
    send_att, recv_a, sum_a, recv_b, near_buf, recv_c, far_buf, recv_d,
    local_sem, send_n, got_n, send_w, got_w,
):
    w = lax.axis_index("wide")
    n = lax.axis_index("narrow")
    mesh_id = pl.DeviceIdType.MESH
    own = pl.ds(pl.multiple_of(n * 256, 256), 256)
    moves = [
        (after_hbm, after_ref), (att_hbm, att_ref), (pos_hbm, pos_ref), (rng_hbm, rng_ref),
        (knot_hbm, knot_ref), (cal_hbm, cal_ref), (unit_hbm, unit_ref),
        (inverse_ref.at[0, own], g_ref), (decay_hbm, decay_ref),
    ]
    loads = [pltpu.make_async_copy(a, b, local_sem.at[k]) for k, (a, b) in enumerate(moves)]
    for load in loads:
        load.start()

    barrier = pltpu.get_barrier_semaphore()
    narrow_to = [lax.rem(n + i, narrow) for i in range(narrow)]
    wide_to = [lax.rem(w + i, wide) for i in range(wide)]
    for i in range(1, narrow):
        pl.semaphore_signal(barrier, inc=1, device_id=(w, narrow_to[i]), device_id_type=mesh_id)
    for i in range(1, wide):
        pl.semaphore_signal(barrier, inc=1, device_id=(wide_to[i], n), device_id_type=mesh_id)

    sent = []

    class Step:
        def __init__(self, along_wide, at, source, slots):
            self.to = wide_to if along_wide else narrow_to
            self.me = w if along_wide else n
            self.out_sem = (send_w if along_wide else send_n).at[at]
            self.in_sem = (got_w if along_wide else got_n).at[at]
            self.along_wide, self.source, self.slots = along_wide, source, slots

        def copy(self, i, slot):
            d = self.to[i]
            return pltpu.make_async_remote_copy(
                src_ref=self.source(d), dst_ref=self.slots.at[slot],
                send_sem=self.out_sem.at[i], recv_sem=self.in_sem.at[slot],
                device_id=(d, n) if self.along_wide else (w, d), device_id_type=mesh_id,
            )

        def start(self):
            for i in range(1, len(self.to)):
                copy = self.copy(i, self.me)
                copy.start()
                sent.append(copy)

        def wait(self):
            for i in range(1, len(self.to)):
                self.copy(i, self.to[i]).wait_recv()

        def total(self):
            self.wait()
            value = self.slots[0]
            for k in range(1, len(self.to)):
                value = value + self.slots[k]
            return value

    iota_ref[...] = lax.broadcasted_iota(jnp.int32, (256, 128), 0).astype(F32).astype(BF16)
    acc_att[...] = jnp.zeros_like(acc_att)
    acc_cal[...] = jnp.zeros_like(acc_cal)
    wide_slots = 2 * SLOT_BLK
    sub8 = lax.broadcasted_iota(jnp.int32, (8, wide_slots), 0)
    first = sub8 < 4
    per = CAL // (narrow * SPLIT)
    per_row = 4 * per
    zero = jnp.zeros((), BF16)
    one = jnp.ones((), BF16)

    def horner(u, low, high):
        c = [jnp.where(first, low[i], high[i]) for i in range(4)]
        return c[0] + u * (c[1] + u * (c[2] + u * c[3]))

    def masked(ids, r, parts):
        here = ids == jnp.asarray(r, BF16)
        return [jnp.where(here, parts[k:k + 16], zero) for k in (0, 16)]

    def summed(acc, ids, count, pieces, place):
        ids = jnp.broadcast_to(ids.astype(F32).astype(BF16), (16, wide_slots))
        left = jnp.concatenate([v for r in range(count) for v in masked(ids, r, pieces)], axis=0)
        grid = jnp.concatenate([iota_ref[...]] * (wide_slots // 128), axis=1)
        hot = jnp.where(grid == place.astype(F32).astype(BF16), one, zero)
        acc[...] += lax.dot_general(left, hot, NT, preferred_element_type=F32)

    def attitude(t, carry):
        cols = pl.ds(pl.multiple_of(t * wide_slots, 128), wide_slots)
        after = jnp.broadcast_to(after_ref[:, cols], (8, wide_slots))
        u = jnp.broadcast_to(pos_ref[:, cols], (8, wide_slots))
        sixth = 1.0 / 6.0
        w01 = horner(u, (sixth, -0.5, 0.5, -sixth), (4.0 / 6.0, 0.0, -1.0, 0.5))
        w23 = horner(u, (sixth, 0.5, 0.5, -0.5), (0.0, 0.0, 0.0, sixth))
        att = att_ref[:, cols]
        scaled = jnp.concatenate([att, att], axis=0) * after
        terms = jnp.concatenate([scaled * w01, scaled * w23], axis=0)
        hi = terms.astype(BF16)
        pieces = jnp.concatenate([hi, (terms - hi.astype(F32)).astype(BF16)], axis=0)
        summed(acc_att, rng_ref[:, cols], wide, pieces, knot_ref[:, cols])
        return carry

    def calibration(t, carry):
        cols = pl.ds(pl.multiple_of(t * wide_slots, 128), wide_slots)
        slot = lax.broadcasted_iota(jnp.int32, (1, SLOT_BLK), 1)
        live = jnp.concatenate([slot < count_ref[2 * t], slot < count_ref[2 * t + 1]], axis=1)
        cal = jnp.where(live, cal_ref[:, cols], 0.0)
        four = jnp.concatenate([cal, after_ref[:, cols]], axis=0)
        f = jnp.concatenate([four, four], axis=0)
        near = f * jnp.where(first, f, pltpu.roll(f, 1, axis=0))
        far = f * pltpu.roll(f, 2, axis=0)
        far_hi, far_mid, far_lo = split3(far)
        far = jnp.where(sub8 < 2, far_hi, jnp.where(first, far_mid, jnp.where(sub8 < 6, far_lo, 0.0)))
        pieces = jnp.concatenate(list(split3(near)) + [far], axis=0).astype(BF16)
        unit = unit_ref[:, cols]
        upper = (unit * ((1 << 22) // per_row + 1)) >> 22
        place = unit - upper * per_row
        late = [jnp.where(place >= q * per, 64 - per, 0) for q in range(1, 4)]
        place = place + (late[0] + late[1] + late[2])
        summed(acc_cal, upper, narrow * 2, pieces, place)
        return carry

    def both(t, carry):
        return calibration(t, attitude(t, carry))

    for load in loads[0:7]:
        load.wait()
    lax.fori_loop(0, blocks // 2, both, 0, unroll=4)

    low = lax.broadcasted_iota(jnp.int32, (5, 128), 1) < 64
    units = []
    for pair in range(narrow * SPLIT // 2):
        top, half = pair // 2, (pair % 2) * 128
        part = acc_cal[top * 32:(top + 1) * 32, half:half + 128]
        near = part[0:8] + part[8:16] + part[16:24]
        far = part[24:26] + part[26:28] + part[28:30]
        upper5 = near[0:5]
        lower5 = jnp.concatenate([near[5:8], far], axis=0)
        units.append(jnp.where(low, upper5, pltpu.roll(lower5, 64, axis=1)))
        units.append(jnp.where(low, pltpu.roll(upper5, 64, axis=1), lower5))
    lane = lax.broadcasted_iota(jnp.int32, (4, 256), 1)
    before = None
    for r in range(wide):
        part = acc_att[r * 32:r * 32 + 16, :] + acc_att[r * 32 + 16:r * 32 + 32, :]
        rolled = [part[0:4]] + [pltpu.roll(part[4 * k:4 * k + 4], k, axis=1) for k in range(1, 4)]
        total = rolled[0]
        for k in range(1, 4):
            wrapped = jnp.zeros((4, 256), F32) if before is None else before[k]
            total = total + jnp.where(lane >= k, rolled[k], wrapped)
        before = rolled
        for k in range(narrow):
            send_att[k, r] = jnp.concatenate(
                [
                    total[k:k + 1, 0:128], total[k:k + 1, 128:256], units[k * SPLIT + r % SPLIT],
                    jnp.zeros((1, 128), F32),
                ],
                axis=0,
            )
    pl.semaphore_wait(barrier, narrow + wide - 2)
    step_a = Step(False, 0, lambda d: send_att.at[d], recv_a)
    step_a.start()
    recv_a[n] = send_att[n]
    sum_a[...] = step_a.total()
    step_b = Step(True, 0, lambda d: sum_a.at[d], recv_b)
    step_b.start()
    recv_b[w] = sum_a[w]

    total = step_b.total()
    for load in loads[7:]:
        load.wait()
    columns = total.T
    y = jnp.zeros((8, 1024), F32)
    for r in range(2):
        prod = columns[:, r:r + 1] * g_ref[r * 128:(r + 1) * 128, :]
        for j in range(16):
            y = y + prod[j * 8:(j + 1) * 8]
    y = jnp.sum(y, axis=0, keepdims=True)
    value = jnp.concatenate([y[:, c * 256:(c + 1) * 256] for c in range(4)], axis=0)
    mul = decay_ref[...]
    add = jnp.sqrt(1.0 - mul * mul) * value
    step = 1
    while step < 256:
        inside = lane >= step
        add = add + mul * jnp.where(inside, pltpu.roll(add, step, axis=1), 0.0)
        mul = mul * jnp.where(inside, pltpu.roll(mul, step, axis=1), 1.0)
        step *= 2
    near_buf[...] = jnp.concatenate([add[:, 0:128], add[:, 128:256]], axis=0)
    step_c = Step(False, 1, lambda d: near_buf, recv_c)
    step_c.start()
    recv_c[n] = near_buf[...]

    turned = pltpu.roll(total, 64, axis=1)
    q = [total[2 + j:3 + j] for j in range(5)] + [turned[2 + j:3 + j] for j in range(5)]
    pair = {(0, 0): q[0], (1, 1): q[1], (2, 2): q[2], (1, 0): q[5], (2, 1): q[6], (2, 0): q[8]}
    x = ldl_solve(lambda i, j: pair[(i, j)], [q[4], q[9], q[7]])
    x = pltpu.roll(jnp.concatenate(x + [jnp.zeros((5, 128), F32)], axis=0), 64, axis=1)

    whole = step_c.total()
    add = jnp.concatenate([whole[0:4], whole[4:8]], axis=1)
    last = jnp.concatenate(
        [jnp.broadcast_to(add[:, 255:256], (4, 128)), jnp.broadcast_to(mul[:, 255:256], (4, 128))],
        axis=0,
    )
    lane8 = lax.broadcasted_iota(jnp.int32, (8, 128), 1)
    far_buf[...] = jnp.where(lane8 < 64, last, x)
    step_d = Step(True, 1, lambda d: far_buf, recv_d)
    step_d.start()
    recv_d[w] = far_buf[...]

    step_d.wait()
    state = jnp.zeros((4, 128), F32)
    for p in range(wide):
        entry = recv_d[p]
        state = jnp.where(p < w, entry[4:8] * state + entry[0:4], state)
    att_out[...] = add + mul * jnp.broadcast_to(state[:, 0:1], (4, 256))

    base = (w // SPLIT) * SPLIT
    for j in range(SPLIT):
        cal_out[j] = recv_d[base + j]
    for copy in sent:
        copy.wait_send()


def finish_kernel(att_ref, cal_ref, att_out, cal_out):
    att_out[...] = att_ref[...]
    per = cal_out.shape[1] // SPLIT
    cal_out[...] = jnp.concatenate(
        [cal_ref[j, 0:3, 64:64 + per] for j in range(SPLIT)], axis=1
    )


def on_device(
    prefit_resid, source_partials, attitude_partials, spline_position, calib_partials, obs_source,
    block_count, obs_range, obs_knot, obs_unit, given_inverse, knot_decay,
):
    wide = lax.axis_size("wide")
    narrow = lax.axis_size("narrow")
    blocks = block_count.shape[0]
    slots = prefit_resid.shape[0]
    vmem = pl.BlockSpec(memory_space=pltpu.VMEM)
    hbm = pl.BlockSpec(memory_space=pltpu.HBM)
    row = lambda v: v.reshape(1, slots)
    limit = 56 * 1024 * 1024
    dma = pltpu.SemaphoreType.DMA
    ints = pltpu.VMEM((1, slots), jnp.int32)
    floats = pltpu.VMEM((1, slots), F32)
    source_update, after = pl.pallas_call(
        functools.partial(source_kernel, blocks),
        out_shape=(
            jax.ShapeDtypeStruct((5, blocks * SRC_BLK), F32),
            jax.ShapeDtypeStruct((1, slots), F32),
        ),
        in_specs=[pl.BlockSpec(memory_space=pltpu.SMEM)] + [hbm] * 3,
        out_specs=(vmem, vmem),
        scratch_shapes=[
            pltpu.VMEM((8, slots), F32),
            pltpu.VMEM((40 * blocks, 128), F32),
            pltpu.VMEM((8 * blocks, 128), F32),
            pltpu.VMEM((SRC_BLK, 128), BF16),
            floats,
            pltpu.VMEM((5, slots), F32),
            ints,
            dma((3,)),
        ],
        compiler_params=pltpu.CompilerParams(vmem_limit_bytes=limit),
        name="sources",
    )(block_count, row(prefit_resid), source_partials, row(obs_source))
    attitude_raw, cal = pl.pallas_call(
        functools.partial(knots_kernel, blocks, wide, narrow),
        out_shape=(
            jax.ShapeDtypeStruct(knot_decay.shape, F32),
            jax.ShapeDtypeStruct((SPLIT, 8, 128), F32),
        ),
        in_specs=[pl.BlockSpec(memory_space=pltpu.SMEM)] + [hbm] * 9,
        out_specs=(vmem, vmem),
        scratch_shapes=[
            floats,
            pltpu.VMEM((4, slots), F32),
            floats, ints, ints,
            pltpu.VMEM((3, slots), F32),
            ints,
            pltpu.VMEM((256, 1024), F32),
            pltpu.VMEM(knot_decay.shape, F32),
            pltpu.VMEM((256, 128), BF16),
            pltpu.VMEM((wide * 32, 256), F32),
            pltpu.VMEM((narrow * 2 * 32, 256), F32),
            pltpu.VMEM((narrow, wide, 8, 128), F32),
            pltpu.VMEM((narrow, wide, 8, 128), F32),
            pltpu.VMEM((wide, 8, 128), F32),
            pltpu.VMEM((wide, 8, 128), F32),
            pltpu.VMEM((8, 128), F32),
            pltpu.VMEM((narrow, 8, 128), F32),
            pltpu.VMEM((8, 128), F32),
            pltpu.VMEM((wide, 8, 128), F32),
            dma((9,)),
            dma((2, narrow)), dma((2, narrow)), dma((2, wide)), dma((2, wide)),
        ],
        compiler_params=pltpu.CompilerParams(
            collective_id=0, has_side_effects=True, vmem_limit_bytes=limit
        ),
        name="knots_units",
    )(
        block_count, after, attitude_partials, row(spline_position), row(obs_range), row(obs_knot),
        calib_partials, row(obs_unit), given_inverse, knot_decay,
    )
    attitude_update, cal_update = pl.pallas_call(
        finish_kernel,
        out_shape=(
            jax.ShapeDtypeStruct(knot_decay.shape, F32),
            jax.ShapeDtypeStruct((3, CAL // narrow), F32),
        ),
        in_specs=[vmem, vmem],
        out_specs=(vmem, vmem),
        compiler_params=pltpu.CompilerParams(vmem_limit_bytes=56 * 1024 * 1024),
        name="finish",
    )(attitude_raw, cal)
    return (source_update, attitude_update, cal_update)


def solution(mesh):
    both = P(("wide", "narrow"))
    rows = P(None, ("wide", "narrow"))
    placed = (
        both, rows, rows, both, rows, both, both, both, both, both, P("wide", None, None), P(None, "wide"),
    )
    return jax.shard_map(
        on_device,
        mesh=mesh,
        in_specs=placed,
        out_specs=(rows, P(None, "wide"), P(None, "narrow")),
        check_vma=False,
    )
```

```python
import functools

import jax
import jax.numpy as jnp
from jax import lax
from jax.experimental import pallas as pl
from jax.experimental.pallas import tpu as pltpu
from jax.sharding import PartitionSpec as P

SRC_BLK = 128
SLOT_BLK = 640
CAL = 2016
SPLIT = 8
NT = (((1,), (1,)), ((), ()))
F32 = jnp.float32
BF16 = jnp.bfloat16


def source_row(i, j):
    d = i - j
    return d * 8 + i if d <= 4 else 3 * 8 + j


def ldl_solve(matrix, target):
    n = len(target)
    low = [[None] * n for _ in range(n)]
    inv = [None] * n
    for c in range(n):
        scaled = [low[c][b][1] for b in range(c)]
        d = matrix(c, c) + 1.0
        for b in range(c):
            d = d - scaled[b] * low[c][b][0]
        inv[c] = 1.0 / d
        for r in range(c + 1, n):
            v = matrix(r, c)
            for b in range(c):
                v = v - low[r][b][1] * low[c][b][0]
            low[r][c] = (v * inv[c], v)
    z = []
    for r in range(n):
        v = target[r]
        for b in range(r):
            v = v - low[r][b][0] * z[b]
        z.append(v)
    x = [None] * n
    for r in reversed(range(n)):
        v = z[r] * inv[r]
        for b in range(r + 1, n):
            v = v - low[b][r][0] * x[b]
        x[r] = v
    return x


def split3(v):
    hi = v.astype(BF16).astype(F32)
    rest = v - hi
    mid = rest.astype(BF16).astype(F32)
    return hi, mid, rest - mid


def source_kernel(
    blocks,
    count_ref, resid_hbm, sp_hbm, src_hbm,
    update_ref, after_ref,
    e_ref, s_ref, x_ref, iota_ref, resid_ref, sp_ref, src_ref, sems,
):
    moves = [(resid_hbm, resid_ref), (sp_hbm, sp_ref), (src_hbm, src_ref)]
    loads = [pltpu.make_async_copy(a, b, sems.at[k]) for k, (a, b) in enumerate(moves)]
    for load in loads:
        load.start()
    iota_ref[...] = lax.broadcasted_iota(jnp.int32, (SRC_BLK, 128), 0).astype(F32).astype(BF16)
    slot = lax.broadcasted_iota(jnp.int32, (1, SLOT_BLK), 1)
    for load in loads:
        load.wait()

    def normals(b, carry):
        at = pl.multiple_of(b * SLOT_BLK, 128)
        cols = pl.ds(at, SLOT_BLK)
        e = jnp.concatenate(
            [sp_ref[:, cols], resid_ref[:, cols], jnp.zeros((2, SLOT_BLK), F32)], axis=0
        )
        live = jnp.broadcast_to(slot < count_ref[b], (8, SLOT_BLK))
        e = jnp.where(live, e, 0.0)
        e_ref[:, cols] = e
        terms = jnp.concatenate(
            [e * e] + [e * pltpu.roll(e, d, axis=0) for d in range(1, 5)], axis=0
        )
        left = jnp.concatenate(split3(terms), axis=0).astype(BF16)
        src = src_ref[:, cols].astype(F32).astype(BF16)
        grid = jnp.concatenate([iota_ref[0:SRC_BLK, :]] * (SLOT_BLK // 128), axis=1)
        hot = jnp.where(grid == src, jnp.ones((), BF16), jnp.zeros((), BF16))
        sums = lax.dot_general(left, hot, NT, preferred_element_type=F32)
        s_ref[pl.ds(b, 40, stride=blocks), :] = sums[0:40] + sums[40:80] + sums[80:120]
        return carry

    lax.fori_loop(0, blocks, normals, 0, unroll=16)

    group = 16
    for g in range(0, blocks, group):
        def entry(i, j, g=g):
            row = source_row(i, j) * blocks + g
            return s_ref[row:row + group, :]

        x = ldl_solve(entry, [entry(5, j) for j in range(5)])
        for p in range(5):
            x_ref[pl.ds(g * 8 + p, group, stride=8), :] = x[p]
        x_ref[pl.ds(g * 8 + 5, group, stride=8), :] = jnp.full((group, 128), -1.0, F32)
        for p in (6, 7):
            x_ref[pl.ds(g * 8 + p, group, stride=8), :] = jnp.zeros((group, 128), F32)

    wide_slots = 2 * SLOT_BLK

    def residuals(t, carry):
        cols = pl.ds(pl.multiple_of(t * wide_slots, 128), wide_slots)
        src = src_ref[:, cols]
        gathered = []
        for half in range(2):
            b = t * 2 + half
            table = x_ref[pl.ds(pl.multiple_of(b * 8, 8), 8), :]
            update_ref[:, pl.ds(pl.multiple_of(b * 128, 128), 128)] = table[0:5, :]
            for q in range(SLOT_BLK // 128):
                lo = half * SLOT_BLK + q * 128
                ids = jnp.broadcast_to(src[:, lo:lo + 128], (8, 128))
                gathered.append(jnp.take_along_axis(table, ids, axis=1, mode="promise_in_bounds"))
        prod = e_ref[:, cols] * jnp.concatenate(gathered, axis=1)
        prod = prod + pltpu.roll(prod, 4, axis=0)
        prod = prod + pltpu.roll(prod, 2, axis=0)
        prod = prod + pltpu.roll(prod, 1, axis=0)
        after_ref[:, cols] = -prod[0:1, :]
        return carry

    lax.fori_loop(0, blocks // 2, residuals, 0, unroll=8)


def knots_kernel(
    blocks, wide, narrow,
    count_ref, after_hbm, att_hbm, pos_hbm, rng_hbm, knot_hbm, cal_hbm, unit_hbm, inverse_ref, decay_hbm,
    att_out, cal_out,
    after_ref, att_ref, pos_ref, rng_ref, knot_ref, cal_ref, unit_ref, g_ref, decay_ref,
    iota_ref, acc_att, acc_cal,
    send_att, recv_a, sum_a, recv_b, near_buf, recv_c, far_buf, recv_d,
    local_sem, send_n, got_n, send_w, got_w,
):
    w = lax.axis_index("wide")
    n = lax.axis_index("narrow")
    mesh_id = pl.DeviceIdType.MESH
    own = pl.ds(pl.multiple_of(n * 256, 256), 256)
    moves = [
        (after_hbm, after_ref), (att_hbm, att_ref), (pos_hbm, pos_ref), (rng_hbm, rng_ref),
        (knot_hbm, knot_ref), (cal_hbm, cal_ref), (unit_hbm, unit_ref),
        (inverse_ref.at[0, own], g_ref), (decay_hbm, decay_ref),
    ]
    loads = [pltpu.make_async_copy(a, b, local_sem.at[k]) for k, (a, b) in enumerate(moves)]
    for load in loads:
        load.start()

    barrier = pltpu.get_barrier_semaphore()
    narrow_to = [lax.rem(n + i, narrow) for i in range(narrow)]
    wide_to = [lax.rem(w + i, wide) for i in range(wide)]
    for i in range(1, narrow):
        pl.semaphore_signal(barrier, inc=1, device_id=(w, narrow_to[i]), device_id_type=mesh_id)
    for i in range(1, wide):
        pl.semaphore_signal(barrier, inc=1, device_id=(wide_to[i], n), device_id_type=mesh_id)

    sent = []

    class Step:
        def __init__(self, along_wide, at, source, slots):
            self.to = wide_to if along_wide else narrow_to
            self.me = w if along_wide else n
            self.out_sem = (send_w if along_wide else send_n).at[at]
            self.in_sem = (got_w if along_wide else got_n).at[at]
            self.along_wide, self.source, self.slots = along_wide, source, slots

        def copy(self, i, slot):
            d = self.to[i]
            return pltpu.make_async_remote_copy(
                src_ref=self.source(d), dst_ref=self.slots.at[slot],
                send_sem=self.out_sem.at[i], recv_sem=self.in_sem.at[slot],
                device_id=(d, n) if self.along_wide else (w, d), device_id_type=mesh_id,
            )

        def start(self):
            for i in range(1, len(self.to)):
                copy = self.copy(i, self.me)
                copy.start()
                sent.append(copy)

        def wait(self):
            for i in range(1, len(self.to)):
                self.copy(i, self.to[i]).wait_recv()

        def total(self):
            self.wait()
            value = self.slots[0]
            for k in range(1, len(self.to)):
                value = value + self.slots[k]
            return value

    iota_ref[...] = lax.broadcasted_iota(jnp.int32, (256, 128), 0).astype(F32).astype(BF16)
    acc_att[...] = jnp.zeros_like(acc_att)
    acc_cal[...] = jnp.zeros_like(acc_cal)
    wide_slots = 2 * SLOT_BLK
    sub8 = lax.broadcasted_iota(jnp.int32, (8, wide_slots), 0)
    first = sub8 < 4
    per = CAL // (narrow * SPLIT)
    per_row = 4 * per
    zero = jnp.zeros((), BF16)
    one = jnp.ones((), BF16)

    def horner(u, low, high):
        c = [jnp.where(first, low[i], high[i]) for i in range(4)]
        return c[0] + u * (c[1] + u * (c[2] + u * c[3]))

    def masked(ids, r, parts):
        here = ids == jnp.asarray(r, BF16)
        return [jnp.where(here, parts[k:k + 16], zero) for k in (0, 16)]

    def summed(acc, ids, count, pieces, place):
        ids = jnp.broadcast_to(ids.astype(F32).astype(BF16), (16, wide_slots))
        left = jnp.concatenate([v for r in range(count) for v in masked(ids, r, pieces)], axis=0)
        grid = jnp.concatenate([iota_ref[...]] * (wide_slots // 128), axis=1)
        hot = jnp.where(grid == place.astype(F32).astype(BF16), one, zero)
        acc[...] += lax.dot_general(left, hot, NT, preferred_element_type=F32)

    def attitude(t, carry):
        cols = pl.ds(pl.multiple_of(t * wide_slots, 128), wide_slots)
        after = jnp.broadcast_to(after_ref[:, cols], (8, wide_slots))
        u = jnp.broadcast_to(pos_ref[:, cols], (8, wide_slots))
        sixth = 1.0 / 6.0
        w01 = horner(u, (sixth, -0.5, 0.5, -sixth), (4.0 / 6.0, 0.0, -1.0, 0.5))
        w23 = horner(u, (sixth, 0.5, 0.5, -0.5), (0.0, 0.0, 0.0, sixth))
        att = att_ref[:, cols]
        scaled = jnp.concatenate([att, att], axis=0) * after
        terms = jnp.concatenate([scaled * w01, scaled * w23], axis=0)
        hi = terms.astype(BF16)
        pieces = jnp.concatenate([hi, (terms - hi.astype(F32)).astype(BF16)], axis=0)
        summed(acc_att, rng_ref[:, cols], wide, pieces, knot_ref[:, cols])
        return carry

    def calibration(t, carry):
        cols = pl.ds(pl.multiple_of(t * wide_slots, 128), wide_slots)
        slot = lax.broadcasted_iota(jnp.int32, (1, SLOT_BLK), 1)
        live = jnp.concatenate([slot < count_ref[2 * t], slot < count_ref[2 * t + 1]], axis=1)
        cal = jnp.where(live, cal_ref[:, cols], 0.0)
        four = jnp.concatenate([cal, after_ref[:, cols]], axis=0)
        f = jnp.concatenate([four, four], axis=0)
        near = f * jnp.where(first, f, pltpu.roll(f, 1, axis=0))
        far = f * pltpu.roll(f, 2, axis=0)
        far_hi, far_mid, far_lo = split3(far)
        far = jnp.where(sub8 < 2, far_hi, jnp.where(first, far_mid, jnp.where(sub8 < 6, far_lo, 0.0)))
        pieces = jnp.concatenate(list(split3(near)) + [far], axis=0).astype(BF16)
        unit = unit_ref[:, cols]
        upper = (unit * ((1 << 22) // per_row + 1)) >> 22
        place = unit - upper * per_row
        late = [jnp.where(place >= q * per, 64 - per, 0) for q in range(1, 4)]
        place = place + (late[0] + late[1] + late[2])
        summed(acc_cal, upper, narrow * 2, pieces, place)
        return carry

    def both(t, carry):
        return calibration(t, attitude(t, carry))

    for load in loads[0:7]:
        load.wait()
    lax.fori_loop(0, blocks // 2, both, 0, unroll=8)

    low = lax.broadcasted_iota(jnp.int32, (5, 128), 1) < 64
    units = []
    for pair in range(narrow * SPLIT // 2):
        top, half = pair // 2, (pair % 2) * 128
        part = acc_cal[top * 32:(top + 1) * 32, half:half + 128]
        near = part[0:8] + part[8:16] + part[16:24]
        far = part[24:26] + part[26:28] + part[28:30]
        upper5 = near[0:5]
        lower5 = jnp.concatenate([near[5:8], far], axis=0)
        units.append(jnp.where(low, upper5, pltpu.roll(lower5, 64, axis=1)))
        units.append(jnp.where(low, pltpu.roll(upper5, 64, axis=1), lower5))
    lane = lax.broadcasted_iota(jnp.int32, (4, 256), 1)
    before = None
    for r in range(wide):
        part = acc_att[r * 32:r * 32 + 16, :] + acc_att[r * 32 + 16:r * 32 + 32, :]
        rolled = [part[0:4]] + [pltpu.roll(part[4 * k:4 * k + 4], k, axis=1) for k in range(1, 4)]
        total = rolled[0]
        for k in range(1, 4):
            wrapped = jnp.zeros((4, 256), F32) if before is None else before[k]
            total = total + jnp.where(lane >= k, rolled[k], wrapped)
        before = rolled
        for k in range(narrow):
            send_att[k, r] = jnp.concatenate(
                [
                    total[k:k + 1, 0:128], total[k:k + 1, 128:256], units[k * SPLIT + r % SPLIT],
                    jnp.zeros((1, 128), F32),
                ],
                axis=0,
            )
    pl.semaphore_wait(barrier, narrow + wide - 2)
    step_a = Step(False, 0, lambda d: send_att.at[d], recv_a)
    step_a.start()
    recv_a[n] = send_att[n]
    sum_a[...] = step_a.total()
    step_b = Step(True, 0, lambda d: sum_a.at[d], recv_b)
    step_b.start()
    recv_b[w] = sum_a[w]

    total = step_b.total()
    for load in loads[7:]:
        load.wait()
    columns = total.T
    y = jnp.zeros((8, 1024), F32)
    for r in range(2):
        prod = columns[:, r:r + 1] * g_ref[r * 128:(r + 1) * 128, :]
        for j in range(16):
            y = y + prod[j * 8:(j + 1) * 8]
    y = jnp.sum(y, axis=0, keepdims=True)
    value = jnp.concatenate([y[:, c * 256:(c + 1) * 256] for c in range(4)], axis=0)
    mul = decay_ref[...]
    add = jnp.sqrt(1.0 - mul * mul) * value
    step = 1
    while step < 256:
        inside = lane >= step
        add = add + mul * jnp.where(inside, pltpu.roll(add, step, axis=1), 0.0)
        mul = mul * jnp.where(inside, pltpu.roll(mul, step, axis=1), 1.0)
        step *= 2
    near_buf[...] = jnp.concatenate([add[:, 0:128], add[:, 128:256]], axis=0)
    step_c = Step(False, 1, lambda d: near_buf, recv_c)
    step_c.start()
    recv_c[n] = near_buf[...]

    turned = pltpu.roll(total, 64, axis=1)
    q = [total[2 + j:3 + j] for j in range(5)] + [turned[2 + j:3 + j] for j in range(5)]
    pair = {(0, 0): q[0], (1, 1): q[1], (2, 2): q[2], (1, 0): q[5], (2, 1): q[6], (2, 0): q[8]}
    x = ldl_solve(lambda i, j: pair[(i, j)], [q[4], q[9], q[7]])
    x = pltpu.roll(jnp.concatenate(x + [jnp.zeros((5, 128), F32)], axis=0), 64, axis=1)

    whole = step_c.total()
    add = jnp.concatenate([whole[0:4], whole[4:8]], axis=1)
    last = jnp.concatenate(
        [jnp.broadcast_to(add[:, 255:256], (4, 128)), jnp.broadcast_to(mul[:, 255:256], (4, 128))],
        axis=0,
    )
    lane8 = lax.broadcasted_iota(jnp.int32, (8, 128), 1)
    far_buf[...] = jnp.where(lane8 < 64, last, x)
    step_d = Step(True, 1, lambda d: far_buf, recv_d)
    step_d.start()
    recv_d[w] = far_buf[...]

    step_d.wait()
    state = jnp.zeros((4, 128), F32)
    for p in range(wide):
        entry = recv_d[p]
        state = jnp.where(p < w, entry[4:8] * state + entry[0:4], state)
    att_out[...] = add + mul * jnp.broadcast_to(state[:, 0:1], (4, 256))

    base = (w // SPLIT) * SPLIT
    for j in range(SPLIT):
        cal_out[j] = recv_d[base + j]
    for copy in sent:
        copy.wait_send()


def finish_kernel(att_ref, cal_ref, att_out, cal_out):
    att_out[...] = att_ref[...]
    per = cal_out.shape[1] // SPLIT
    cal_out[...] = jnp.concatenate(
        [cal_ref[j, 0:3, 64:64 + per] for j in range(SPLIT)], axis=1
    )


def on_device(
    prefit_resid, source_partials, attitude_partials, spline_position, calib_partials, obs_source,
    block_count, obs_range, obs_knot, obs_unit, given_inverse, knot_decay,
):
    wide = lax.axis_size("wide")
    narrow = lax.axis_size("narrow")
    blocks = block_count.shape[0]
    slots = prefit_resid.shape[0]
    vmem = pl.BlockSpec(memory_space=pltpu.VMEM)
    hbm = pl.BlockSpec(memory_space=pltpu.HBM)
    row = lambda v: v.reshape(1, slots)
    limit = 56 * 1024 * 1024
    dma = pltpu.SemaphoreType.DMA
    ints = pltpu.VMEM((1, slots), jnp.int32)
    floats = pltpu.VMEM((1, slots), F32)
    source_update, after = pl.pallas_call(
        functools.partial(source_kernel, blocks),
        out_shape=(
            jax.ShapeDtypeStruct((5, blocks * SRC_BLK), F32),
            jax.ShapeDtypeStruct((1, slots), F32),
        ),
        in_specs=[pl.BlockSpec(memory_space=pltpu.SMEM)] + [hbm] * 3,
        out_specs=(vmem, vmem),
        scratch_shapes=[
            pltpu.VMEM((8, slots), F32),
            pltpu.VMEM((40 * blocks, 128), F32),
            pltpu.VMEM((8 * blocks, 128), F32),
            pltpu.VMEM((SRC_BLK, 128), BF16),
            floats,
            pltpu.VMEM((5, slots), F32),
            ints,
            dma((3,)),
        ],
        compiler_params=pltpu.CompilerParams(vmem_limit_bytes=limit),
        name="sources",
    )(block_count, row(prefit_resid), source_partials, row(obs_source))
    attitude_raw, cal = pl.pallas_call(
        functools.partial(knots_kernel, blocks, wide, narrow),
        out_shape=(
            jax.ShapeDtypeStruct(knot_decay.shape, F32),
            jax.ShapeDtypeStruct((SPLIT, 8, 128), F32),
        ),
        in_specs=[pl.BlockSpec(memory_space=pltpu.SMEM)] + [hbm] * 9,
        out_specs=(vmem, vmem),
        scratch_shapes=[
            floats,
            pltpu.VMEM((4, slots), F32),
            floats, ints, ints,
            pltpu.VMEM((3, slots), F32),
            ints,
            pltpu.VMEM((256, 1024), F32),
            pltpu.VMEM(knot_decay.shape, F32),
            pltpu.VMEM((256, 128), BF16),
            pltpu.VMEM((wide * 32, 256), F32),
            pltpu.VMEM((narrow * 2 * 32, 256), F32),
            pltpu.VMEM((narrow, wide, 8, 128), F32),
            pltpu.VMEM((narrow, wide, 8, 128), F32),
            pltpu.VMEM((wide, 8, 128), F32),
            pltpu.VMEM((wide, 8, 128), F32),
            pltpu.VMEM((8, 128), F32),
            pltpu.VMEM((narrow, 8, 128), F32),
            pltpu.VMEM((8, 128), F32),
            pltpu.VMEM((wide, 8, 128), F32),
            dma((9,)),
            dma((2, narrow)), dma((2, narrow)), dma((2, wide)), dma((2, wide)),
        ],
        compiler_params=pltpu.CompilerParams(
            collective_id=0, has_side_effects=True, vmem_limit_bytes=limit
        ),
        name="knots_units",
    )(
        block_count, after, attitude_partials, row(spline_position), row(obs_range), row(obs_knot),
        calib_partials, row(obs_unit), given_inverse, knot_decay,
    )
    attitude_update, cal_update = pl.pallas_call(
        finish_kernel,
        out_shape=(
            jax.ShapeDtypeStruct(knot_decay.shape, F32),
            jax.ShapeDtypeStruct((3, CAL // narrow), F32),
        ),
        in_specs=[vmem, vmem],
        out_specs=(vmem, vmem),
        compiler_params=pltpu.CompilerParams(vmem_limit_bytes=56 * 1024 * 1024),
        name="finish",
    )(attitude_raw, cal)
    return (source_update, attitude_update, cal_update)


def solution(mesh):
    both = P(("wide", "narrow"))
    rows = P(None, ("wide", "narrow"))
    placed = (
        both, rows, rows, both, rows, both, both, both, both, both, P("wide", None, None), P(None, "wide"),
    )
    return jax.shard_map(
        on_device,
        mesh=mesh,
        in_specs=placed,
        out_specs=(rows, P(None, "wide"), P(None, "narrow")),
        check_vma=False,
    )
```
